32 devices in a mesh: pairs: 2 (over x), src: 8 (over z, y), tgt: 2 (over core).
Axes of the slice: x: 2, y: 2, z: 4, core: 2. Of those that a mesh axis runs over, the one named last changes fastest.
Arguments:
- src_feat: float32 [2048, 32], P(('pairs', 'src'), 'tgt'), parts along dimension 0, may hold values from -0.72 to 0.72
- tgt_feat: float32 [32768, 32], P(('pairs', 'tgt'), 'src'), parts along dimension 0, may hold values from -0.72 to 0.72
- tgt_dual: float32 [32768], P(('pairs', 'tgt')), parts along dimension 0, may hold values from -6 to 6
- core_matrix: float32 [68, 34], P('pairs'), parts along dimension 0, may hold values from -3 to 3
Outputs:
- src_dual: float32 [2048], P(('pairs', 'src')), parts along dimension 0
- tgt_dual_out: float32 [32768], P(('pairs', 'tgt')), parts along dimension 0
- core_out: float32 [68, 34], P('pairs'), parts along dimension 0
The draws below stay inside these ranges and needn't reach their ends.
There are 2 independent parts, one for each index of `pairs`. The reference program is written for one: setup_inputs(seed, part) draws one part's arguments, and reference() takes and returns one part's arrays. A program takes and returns all parts, laid end to end along the dimension named above; each array names one. Nothing has to cross between parts.
All inputs are finite; a program needn't handle non-finite values.
Results may differ from the reference program's by a relative error of at most 0.0003.
Values sent between devices are 32-bit elements; how exact they have to be, the bound alone decides.
A program may use at most 64 MiB of HBM per device.

```python
import jax
import jax.numpy as jnp
from jax import lax

FEAT = 32
RANK = 34
RS = 128
OUTER = 2
NS = 1024
NT = 16384


def block_levels(rng, dims, cuts, smallest, largest):
    level = 1.0
    for dim, shards_of in cuts:
        steps = jax.random.uniform(jax.random.fold_in(jax.random.fold_in(rng, 6), dim), (shards_of,), jnp.float32, smallest / len(cuts), largest / len(cuts))
        level = level * jnp.repeat(jnp.exp(steps), dims[dim] // shards_of).reshape((-1,) + (1,) * (len(dims) - 1 - dim))
    return level


def bell_draw(stream_key, dims, scale, reach, split=(), dtype=jnp.bfloat16):
    array = scale * jax.random.normal(stream_key, dims, jnp.float32)
    if split:
        array = array * block_levels(stream_key, dims, split, -0.22, 0.18)
    return jnp.clip(array, -reach, reach).astype(dtype)


def setup_inputs(seed: int = 0, part: int = 0) -> dict:
    seeds = jax.random.split(jax.random.key(seed), 5)
    own_keys = jax.random.split(jax.random.fold_in(seeds[4], part), 5)
    return {
        "src_feat": bell_draw(own_keys[0], (NS, FEAT), 0.12, 0.72, ((0, 8), (1, 2)), jnp.float32),
        "tgt_feat": bell_draw(own_keys[1], (NT, FEAT), 0.12, 0.72, ((0, 2), (1, 8)), jnp.float32),
        "tgt_dual": bell_draw(own_keys[2], (NT,), 1.0, 6.0, ((0, 2),), jnp.float32),
        "core_matrix": bell_draw(own_keys[3], (RANK, RANK), 0.5, 3.0, (), jnp.float32),
    }


EPSILON = 0.02
HIGH = lax.Precision.HIGHEST


def lifted(values):
    squares = jnp.sum(values * values, axis=1, keepdims=True)
    ones = jnp.ones_like(squares)
    left = jnp.concatenate([squares, ones, -2.0 * values], axis=1)
    right = jnp.concatenate([ones, squares, values], axis=1)
    return left, right


def merge_logsum(earlier, later):
    top = jnp.maximum(earlier[0], later[0])
    return (top, earlier[1] * jnp.exp(earlier[0] - top) + later[1] * jnp.exp(later[0] - top))


def reference(src_feat, tgt_feat, tgt_dual, core_matrix):
    src_left, src_right = lifted(src_feat)
    tgt_left, tgt_right = lifted(tgt_feat)
    log_src = -jnp.log(jnp.float32(NS))
    log_tgt = -jnp.log(jnp.float32(NT))
    blocks = NS // RS
    right_blocks = src_right.reshape(blocks, RS, RANK)
    src_dual = jnp.zeros((NS,), jnp.float32)
    for outer_step in range(OUTER):
        projected = jnp.dot(src_left, core_matrix, precision=HIGH).reshape(blocks, RS, RANK)

        def row_block(proj):
            linear = jnp.dot(proj, tgt_right.T, precision=HIGH)
            logits = (tgt_dual[None, :] - linear) / EPSILON
            top = jnp.max(logits, axis=1)
            total = jnp.sum(jnp.exp(logits - top[:, None]), axis=1)
            return EPSILON * log_src - EPSILON * (top + jnp.log(total))

        src_dual = lax.map(row_block, projected).reshape(NS)
        dual_blocks = src_dual.reshape(blocks, RS)

        def col_block(carry, inputs):
            proj, duals = inputs
            linear = jnp.dot(proj, tgt_right.T, precision=HIGH)
            logits = (duals[:, None] - linear) / EPSILON
            top = jnp.max(logits, axis=0)
            total = jnp.sum(jnp.exp(logits - top[None, :]), axis=0)
            return merge_logsum(carry, (top, total)), None

        start = (jnp.full((NT,), -jnp.inf, jnp.float32), jnp.zeros((NT,), jnp.float32))
        (top, total), unused = lax.scan(col_block, start, (projected, dual_blocks))
        tgt_dual = EPSILON * log_tgt - EPSILON * (top + jnp.log(total))

        def core_block(carry, inputs):
            proj, duals, right = inputs
            linear = jnp.dot(proj, tgt_right.T, precision=HIGH)
            coupling = jnp.exp((duals[:, None] + tgt_dual[None, :] - linear) / EPSILON)
            weighted = jnp.dot(coupling, tgt_left, precision=HIGH)
            return carry + jnp.dot(right.T, weighted, precision=HIGH), None

        core_sum, unused = lax.scan(core_block, jnp.zeros((RANK, RANK), jnp.float32),
                                    (projected, dual_blocks, right_blocks))
        core_matrix = -2.0 * core_sum
    return src_dual, tgt_dual, core_matrix
```

```python
import functools
import math

import jax
import jax.numpy as jnp
from jax import lax
from jax.experimental import pallas as pl
from jax.experimental.pallas import tpu as pltpu
from jax.sharding import PartitionSpec as P

OUTER = 2
EPSILON = 0.02
LOG2E = math.log2(math.e)
UNIT = EPSILON / LOG2E
LANES = 128
MESH = pl.DeviceIdType.MESH
BF16 = jnp.bfloat16
F32 = jnp.float32


def split3(x):
    high = x.astype(BF16).astype(F32)
    rest = x - high
    mid = rest.astype(BF16).astype(F32)
    return high, mid, rest - mid


def lanes_below(x, count):
    return jnp.where(lax.broadcasted_iota(jnp.int32, x.shape, 1) < count, x, 0.0)


def shifted(x, by):
    return x if by % LANES == 0 else pltpu.roll(x, by % LANES, 1)


def kernel(
    dims, src_ref, tgt_ref, dual_ref, core_ref, u_out, g_out, core_out,
    srcbuf, tgtbuf, lsebuf, corebuf, gbuf, sl, sr, tl, tr, sls, srs, tls, trt, sps, logits, gcol, weighted, urow, square,
    send_sem, recv_sem,
):
    S, T, rows, cols, fs, ft, feat, ns, nt = dims
    D = S * T
    rank = feat + 2
    st = -(-rank // 8) * 8
    jr = cols // LANES
    nr = rows // LANES
    s, t = lax.axis_index("src"), lax.axis_index("tgt")
    me = s * T + t

    def everyone(act):
        def body(k, unused):
            peer = lax.rem(me + k, D)
            act(peer, peer // T, lax.rem(peer, T))
            return unused

        lax.fori_loop(1, D, body, 0)

    def column(act):
        def body(k, unused):
            act(lax.rem(s + k, S))
            return unused

        lax.fori_loop(1, S, body, 0)

    def remote(phase, src, dst, out_id, in_id, device):
        return pltpu.make_async_remote_copy(
            src_ref=src, dst_ref=dst, send_sem=send_sem.at[phase, out_id], recv_sem=recv_sem.at[phase, in_id],
            device_id=device, device_id_type=MESH,
        )

    def share(phase, buf, k):
        def act(peer, ps, pt):
            remote(phase, buf.at[k, me], buf.at[k, me], peer, me, {"src": ps, "tgt": pt}).start()

        everyone(act)

    def shared(phase, buf, k):
        def act(peer, ps, pt):
            remote(phase, buf.at[k, peer], buf.at[k, peer], peer, peer, {"src": ps, "tgt": pt}).wait_recv()

        everyone(act)

    def sent(phase, buf, k):
        def act(peer, ps, pt):
            remote(phase, buf.at[k, me], buf.at[k, me], peer, me, {"src": ps, "tgt": pt}).wait_send()

        everyone(act)

    barrier = pltpu.get_barrier_semaphore()

    def greet(peer, ps, pt):
        pl.semaphore_signal(barrier, inc=1, device_id={"src": ps, "tgt": pt}, device_id_type=MESH)

    everyone(greet)
    srcbuf[s, t] = src_ref[...]
    tgtbuf[s] = tgt_ref[s]
    own_dual = dual_ref[s] * (1.0 / UNIT)
    for r in range(jr):
        gcol[r * LANES : (r + 1) * LANES, :] = jnp.broadcast_to(own_dual[r : r + 1, :], (LANES, LANES)).T
    square[...] = jnp.zeros_like(square)
    square[:rank, :rank] = core_ref[...]
    turned = square[...].T[:st, :]
    pl.semaphore_wait(barrier, D - 1)

    def send_tgt(ps):
        remote(1, tgt_ref.at[ps], tgtbuf.at[s], ps, s, {"src": ps}).start()

    column(send_tgt)

    def send_src(peer, ps, pt):
        remote(0, src_ref, srcbuf.at[s, t], peer, me, {"src": ps, "tgt": pt}).start()

    everyone(send_src)

    def get_tgt(ps):
        remote(1, tgt_ref.at[ps], tgtbuf.at[ps], ps, ps, {"src": ps}).wait_recv()

    column(get_tgt)

    def lift(left, right):
        values = right[2:rank, :]
        squares = jnp.sum(values * values, axis=0, keepdims=True)
        ones = jnp.ones_like(squares)
        left[rank:, :] = jnp.zeros_like(left[rank:, :])
        right[rank:, :] = jnp.zeros_like(right[rank:, :])
        left[0:1, :] = squares
        left[1:2, :] = ones
        left[2:rank, :] = -2.0 * values
        right[0:1, :] = ones
        right[1:2, :] = squares

    def stacked(parts, height):
        width = parts[0].shape[1]
        fill = height - st * len(parts)
        return jnp.concatenate(list(parts) + ([jnp.zeros((fill, width), F32)] if fill else []), axis=0)

    deep = trt.shape[1]
    wide = srs.shape[1]
    for k in range(S):
        for r in range(jr):
            tr[2 + k * ft : 2 + (k + 1) * ft, r * LANES : (r + 1) * LANES] = tgtbuf[k, r * ft : (r + 1) * ft, :]
    lift(tl, tr)
    t0, t1, t2 = split3(tr[...])
    trt[...] = stacked((t0, t1, t0, t1, t2, t0), deep).T.astype(BF16)
    tls[...] = stacked(split3(tl[...]), wide).astype(BF16)

    def get_src(peer, ps, pt):
        remote(0, src_ref, srcbuf.at[ps, pt], peer, peer, {"src": ps, "tgt": pt}).wait_recv()

    everyone(get_src)
    for k in range(S):
        for h in range(T):
            sr[2 + h * fs : 2 + (h + 1) * fs, k * rows : (k + 1) * rows] = srcbuf[k, h]
    lift(sl, sr)
    sls[...] = stacked(split3(sl[...]), wide).astype(BF16)
    srs[...] = stacked(split3(sr[...]), wide).T.astype(BF16)

    per = LANES // st
    block = min(256, ns)
    chunk = min(256, cols)
    for step in range(OUTER):
        k0, k1, k2 = split3(turned * (-1.0 / UNIT))
        lhs = stacked(
            (k0 + shifted(k0, st) + shifted(k0, 2 * st), k1 + shifted(k1, st), k2), 3 * st
        ).astype(BF16)
        proj = jnp.dot(lhs, sls[...], preferred_element_type=F32)
        proj = proj[:st] + (proj[st : 2 * st] + proj[2 * st :])
        p0, p1, p2 = split3(proj)
        sps[...] = stacked((p0, p0, p1, p1, p0, p2), deep).astype(BF16)
        for b in range(ns // block):
            part = jnp.dot(trt[...], sps[:, b * block : (b + 1) * block], preferred_element_type=F32)
            for h in range(block // LANES):
                at = b * block // LANES + h
                here = part[:, h * LANES : (h + 1) * LANES] + gcol[...]
                logits[:, at * LANES : (at + 1) * LANES] = here
                top = jnp.max(here, axis=0, keepdims=True)
                total = jnp.sum(jnp.exp2(here - top), axis=0, keepdims=True)
                lsebuf[step, me, at : at + 1, :] = top + jnp.log2(total)
        share(2 + 2 * step, lsebuf, step)
        shared(2 + 2 * step, lsebuf, step)
        top = jnp.max(lsebuf[step], axis=0)
        total = jnp.sum(jnp.exp2(lsebuf[step] - top[None]), axis=0)
        urow[...] = -math.log2(ns) - (top + jnp.log2(total))
        u_all = jnp.concatenate([urow[k : k + 1, :] for k in range(ns // LANES)], axis=1)
        for c in range(cols // chunk):
            sl_c = slice(c * chunk, (c + 1) * chunk)
            x = logits[sl_c, :] + u_all
            top = jnp.max(x, axis=1, keepdims=True)
            e = jnp.exp2(x - top)
            high = e.astype(BF16)
            low = (e - high.astype(F32)).astype(BF16)
            acc = jnp.dot(high, srs[...], preferred_element_type=F32) + jnp.dot(low, srs[...], preferred_element_type=F32)
            total = acc[:, 0:1]
            scaled = acc * (1.0 / total)
            first = scaled.astype(BF16)
            weighted[sl_c, :wide] = first
            weighted[sl_c, wide:] = (scaled - first.astype(F32)).astype(BF16)
            gcol[sl_c, :] = (gcol[sl_c, :] - math.log2(nt)) - (top + jnp.log2(total))
        if step == OUTER - 1:
            for r in range(jr):
                gbuf[s, r : r + 1, :] = gcol[r * LANES : (r + 1) * LANES, :].T[0:1, :] * UNIT

            def send_g(ps):
                remote(1 + 2 * OUTER + 1, gbuf.at[s], gbuf.at[s], ps, s, {"src": ps}).start()

            column(send_g)
        ext = jnp.dot(tls[...], weighted[...], preferred_element_type=F32)
        ext = ext[:, :wide] + ext[:, wide:]
        kt = ext[:st] + (ext[st : 2 * st] + ext[2 * st : 3 * st])
        kt = kt + (shifted(kt, -st) + shifted(kt, -2 * st))
        kt = lanes_below(kt * (1.0 / nt), st)
        for group in range(corebuf.shape[2] // 8):
            tile = None
            for k in range(per):
                n = group * per + k
                if n * 8 < st:
                    piece = shifted(kt[n * 8 : n * 8 + 8, :], k * st)
                    tile = piece if tile is None else tile + piece
            corebuf[step, me, group * 8 : group * 8 + 8, :] = tile
        share(3 + 2 * step, corebuf, step)
        shared(3 + 2 * step, corebuf, step)
        summed = -2.0 * jnp.sum(corebuf[step], axis=0)
        turned = jnp.concatenate(
            [
                lanes_below(shifted(summed[n // per * 8 : n // per * 8 + 8, :], -(n % per) * st), st)
                for n in range(st // 8)
            ],
            axis=0,
        )
    u_out[...] = urow[pl.ds(s * nr, nr), :] * UNIT
    square[:st, :] = turned
    core_out[...] = square[...].T[:rank, :rank]

    def get_g(ps):
        remote(1 + 2 * OUTER + 1, gbuf.at[ps], gbuf.at[ps], ps, ps, {"src": ps}).wait_recv()

    column(get_g)
    g_out[...] = gbuf[...]

    def done_tgt(ps):
        remote(1, tgt_ref.at[ps], tgtbuf.at[s], ps, s, {"src": ps}).wait_send()
        remote(1 + 2 * OUTER + 1, gbuf.at[s], gbuf.at[s], ps, s, {"src": ps}).wait_send()

    column(done_tgt)

    def done_src(peer, ps, pt):
        remote(0, src_ref, srcbuf.at[s, t], peer, me, {"src": ps, "tgt": pt}).wait_send()

    everyone(done_src)
    for step in range(OUTER):
        sent(2 + 2 * step, lsebuf, step)
        sent(3 + 2 * step, corebuf, step)


def shards(src_feat, tgt_feat, tgt_dual, core_matrix):
    S, T = lax.axis_size("src"), lax.axis_size("tgt")
    D = S * T
    rows, fs = src_feat.shape
    held, ft = tgt_feat.shape
    feat = fs * T
    cols = held // S
    ns, nt = rows * S, held * T
    rank = feat + 2
    st = -(-rank // 8) * 8
    jr, nr = cols // LANES, rows // LANES
    per = LANES // st
    groups = -(-(st // 8) // per)
    deep = -(-6 * st // LANES) * LANES
    wide = -(-3 * st // LANES) * LANES
    dims = (S, T, rows, cols, fs, ft, feat, ns, nt)
    src = src_feat.T
    tgt = tgt_feat.reshape(S * jr, LANES, ft).transpose(0, 2, 1).reshape(S, jr * ft, LANES)
    dual = tgt_dual.reshape(S, jr, LANES)
    phases = 2 + 2 * OUTER + 1
    vmem = pl.BlockSpec(memory_space=pltpu.VMEM)
    u, g, core = pl.pallas_call(
        functools.partial(kernel, dims),
        out_shape=(
            jax.ShapeDtypeStruct((nr, LANES), F32),
            jax.ShapeDtypeStruct((S, jr, LANES), F32),
            jax.ShapeDtypeStruct((rank, rank), F32),
        ),
        in_specs=[vmem] * 4,
        out_specs=(vmem,) * 3,
        scratch_shapes=[
            pltpu.VMEM((S, T, fs, rows), F32),
            pltpu.VMEM((S, jr * ft, LANES), F32),
            pltpu.VMEM((OUTER, D, ns // LANES, LANES), F32),
            pltpu.VMEM((OUTER, D, groups * 8, LANES), F32),
            pltpu.VMEM((S, jr, LANES), F32),
            pltpu.VMEM((st, ns), F32),
            pltpu.VMEM((st, ns), F32),
            pltpu.VMEM((st, cols), F32),
            pltpu.VMEM((st, cols), F32),
            pltpu.VMEM((wide, ns), BF16),
            pltpu.VMEM((ns, wide), BF16),
            pltpu.VMEM((wide, cols), BF16),
            pltpu.VMEM((cols, deep), BF16),
            pltpu.VMEM((deep, ns), BF16),
            pltpu.VMEM((cols, ns), F32),
            pltpu.VMEM((cols, LANES), F32),
            pltpu.VMEM((cols, 2 * wide), BF16),
            pltpu.VMEM((ns // LANES, LANES), F32),
            pltpu.VMEM((LANES, LANES), F32),
            pltpu.SemaphoreType.DMA((phases, D)),
            pltpu.SemaphoreType.DMA((phases, D)),
        ],
        compiler_params=pltpu.CompilerParams(
            collective_id=0, has_side_effects=True, vmem_limit_bytes=48 * 1024 * 1024
        ),
    )(src, tgt, dual, core_matrix)
    return u.reshape(rows), g.reshape(held), core


def solution(mesh):
    placed = (
        P(("pairs", "src"), "tgt"),
        P(("pairs", "tgt"), "src"),
        P(("pairs", "tgt")),
        P("pairs", None),
    )
    return jax.shard_map(
        shards,
        mesh=mesh,
        in_specs=placed,
        out_specs=(P(("pairs", "src")), P(("pairs", "tgt")), P("pairs", None)),
        check_vma=False,
    )
```

```python
import functools
import math

import jax
import jax.numpy as jnp
from jax import lax
from jax.experimental import pallas as pl
from jax.experimental.pallas import tpu as pltpu
from jax.sharding import PartitionSpec as P

OUTER = 2
EPSILON = 0.02
LOG2E = math.log2(math.e)
UNIT = EPSILON / LOG2E
LANES = 128
MESH = pl.DeviceIdType.MESH
BF16 = jnp.bfloat16
F32 = jnp.float32


def split3(x):
    high = x.astype(BF16).astype(F32)
    rest = x - high
    mid = rest.astype(BF16).astype(F32)
    return high, mid, rest - mid


def lanes_below(x, count):
    return jnp.where(lax.broadcasted_iota(jnp.int32, x.shape, 1) < count, x, 0.0)


def shifted(x, by):
    return x if by % LANES == 0 else pltpu.roll(x, by % LANES, 1)


def kernel(
    dims, src_ref, tgt_ref, dual_ref, core_ref, u_out, g_out, core_out,
    srcbuf, tgtall, tgtbuf, dualbuf, corein, lsebuf, corebuf, gbuf, sl, sr, tl, tr, sls, srs, tls, trt, sps, logits, gcol, weighted, urow, square,
    send_sem, recv_sem, local_sem,
):
    S, T, rows, cols, fs, ft, feat, ns, nt = dims
    D = S * T
    rank = feat + 2
    st = -(-rank // 8) * 8
    jr = cols // LANES
    nr = rows // LANES
    last = 2 + 2 * OUTER
    s, t = lax.axis_index("src"), lax.axis_index("tgt")
    me = s * T + t

    def everyone(act):
        def body(k, unused):
            ps = lax.rem(s + k, S)
            for h in range(T):
                pt = lax.rem(t + h, T)
                act(ps, pt)
            return unused

        lax.fori_loop(1, S, body, 0, unroll=S <= 8)
        for h in range(1, T):
            act(s, lax.rem(t + h, T))

    def column(act):
        def body(k, unused):
            act(lax.rem(s + k, S))
            return unused

        lax.fori_loop(1, S, body, 0, unroll=S <= 8)

    def remote(phase, src, dst, device):
        return pltpu.make_async_remote_copy(
            src_ref=src, dst_ref=dst, send_sem=send_sem.at[phase], recv_sem=recv_sem.at[phase],
            device_id=device, device_id_type=MESH,
        )

    def share(phase, slots):
        def act(ps, pt):
            remote(phase, slots.at[me], slots.at[me], {"src": ps, "tgt": pt}).start()

        everyone(act)

    def bytes_of(phase, slots, count):
        part = slots.at[pl.ds(0, count - 1)]
        return remote(phase, part, part, {"src": lax.rem(s + 1, S)})

    copies = [
        pltpu.make_async_copy(src_ref, srcbuf.at[me], local_sem.at[0]),
        pltpu.make_async_copy(tgt_ref, tgtall, local_sem.at[1]),
        pltpu.make_async_copy(dual_ref.at[s], dualbuf, local_sem.at[2]),
        pltpu.make_async_copy(core_ref, corein, local_sem.at[3]),
    ]
    for copy in copies:
        copy.start()
    barrier = pltpu.get_barrier_semaphore()

    def greet(ps, pt):
        pl.semaphore_signal(barrier, inc=1, device_id={"src": ps, "tgt": pt}, device_id_type=MESH)

    everyone(greet)
    for copy in copies:
        copy.wait()
    tgtbuf[s] = tgtall[s]
    own_dual = dualbuf[...] * (1.0 / UNIT)
    for r in range(jr):
        gcol[r * LANES : (r + 1) * LANES, :] = jnp.broadcast_to(own_dual[r : r + 1, :], (LANES, LANES)).T
    square[...] = jnp.zeros_like(square)
    square[:rank, :rank] = corein[...]
    turned = square[...].T[:st, :]
    pl.semaphore_wait(barrier, D - 1)

    def send_tgt(ps):
        remote(1, tgtall.at[ps], tgtbuf.at[s], {"src": ps}).start()

    column(send_tgt)

    def send_src(ps, pt):
        remote(0, srcbuf.at[me], srcbuf.at[me], {"src": ps, "tgt": pt}).start()

    everyone(send_src)
    bytes_of(1, tgtbuf, S).wait_recv()

    def lift(left, right):
        values = right[2:rank, :]
        squares = jnp.sum(values * values, axis=0, keepdims=True)
        ones = jnp.ones_like(squares)
        left[rank:, :] = jnp.zeros_like(left[rank:, :])
        right[rank:, :] = jnp.zeros_like(right[rank:, :])
        left[0:1, :] = squares
        left[1:2, :] = ones
        left[2:rank, :] = -2.0 * values
        right[0:1, :] = ones
        right[1:2, :] = squares

    def stacked(parts, height):
        width = parts[0].shape[1]
        fill = height - st * len(parts)
        return jnp.concatenate(list(parts) + ([jnp.zeros((fill, width), F32)] if fill else []), axis=0)

    deep = trt.shape[1]
    wide = srs.shape[1]
    for k in range(S):
        for r in range(jr):
            tr[2 + k * ft : 2 + (k + 1) * ft, r * LANES : (r + 1) * LANES] = tgtbuf[k, r * ft : (r + 1) * ft, :]
    lift(tl, tr)
    t0, t1, t2 = split3(tr[...])
    trt[...] = stacked((t0, t1, t0, t1, t2, t0), deep).T.astype(BF16)
    tls[...] = stacked(split3(tl[...]), wide).astype(BF16)

    bytes_of(0, srcbuf, D).wait_recv()
    for k in range(S):
        for h in range(T):
            sr[2 + h * fs : 2 + (h + 1) * fs, k * rows : (k + 1) * rows] = srcbuf[k * T + h]
    lift(sl, sr)
    sls[...] = stacked(split3(sl[...]), wide).astype(BF16)
    srs[...] = stacked(split3(sr[...]), wide).T.astype(BF16)

    per = LANES // st
    block = min(256, ns)
    chunk = min(256, cols)
    for step in range(OUTER):
        k0, k1, k2 = split3(turned * (-1.0 / UNIT))
        lhs = stacked(
            (k0 + shifted(k0, st) + shifted(k0, 2 * st), k1 + shifted(k1, st), k2), 3 * st
        ).astype(BF16)
        proj = jnp.dot(lhs, sls[...], preferred_element_type=F32)
        proj = proj[:st] + (proj[st : 2 * st] + proj[2 * st :])
        p0, p1, p2 = split3(proj)
        sps[...] = stacked((p0, p0, p1, p1, p0, p2), deep).astype(BF16)
        for b in range(ns // block):
            part = jnp.dot(trt[...], sps[:, b * block : (b + 1) * block], preferred_element_type=F32)
            for h in range(block // LANES):
                at = b * block // LANES + h
                here = part[:, h * LANES : (h + 1) * LANES] + gcol[...]
                logits[:, at * LANES : (at + 1) * LANES] = here
                top = jnp.max(here, axis=0, keepdims=True)
                total = jnp.sum(jnp.exp2(here - top), axis=0, keepdims=True)
                lsebuf[step, me, at : at + 1, :] = top + jnp.log2(total)
        share(2 + 2 * step, lsebuf.at[step])
        bytes_of(2 + 2 * step, lsebuf.at[step], D).wait_recv()
        top = jnp.max(lsebuf[step], axis=0)
        total = jnp.sum(jnp.exp2(lsebuf[step] - top[None]), axis=0)
        urow[...] = -math.log2(ns) - (top + jnp.log2(total))
        u_all = jnp.concatenate([urow[k : k + 1, :] for k in range(ns // LANES)], axis=1)
        for c in range(cols // chunk):
            sl_c = slice(c * chunk, (c + 1) * chunk)
            x = logits[sl_c, :] + u_all
            top = jnp.max(x, axis=1, keepdims=True)
            e = jnp.exp2(x - top)
            high = e.astype(BF16)
            low = (e - high.astype(F32)).astype(BF16)
            acc = jnp.dot(high, srs[...], preferred_element_type=F32) + jnp.dot(low, srs[...], preferred_element_type=F32)
            total = acc[:, 0:1]
            scaled = acc * (1.0 / total)
            first = scaled.astype(BF16)
            weighted[sl_c, :wide] = first
            weighted[sl_c, wide:] = (scaled - first.astype(F32)).astype(BF16)
            gcol[sl_c, :] = (gcol[sl_c, :] - math.log2(nt)) - (top + jnp.log2(total))
        if step == OUTER - 1:
            for r in range(jr):
                gbuf[s, r : r + 1, :] = gcol[r * LANES : (r + 1) * LANES, :].T[0:1, :] * UNIT

            def send_g(ps):
                remote(last, gbuf.at[s], gbuf.at[s], {"src": ps}).start()

            column(send_g)
        ext = jnp.dot(tls[...], weighted[...], preferred_element_type=F32)
        ext = ext[:, :wide] + ext[:, wide:]
        kt = ext[:st] + (ext[st : 2 * st] + ext[2 * st : 3 * st])
        kt = kt + (shifted(kt, -st) + shifted(kt, -2 * st))
        kt = lanes_below(kt * (1.0 / nt), st)
        for group in range(corebuf.shape[2] // 8):
            tile = None
            for k in range(per):
                n = group * per + k
                if n * 8 < st:
                    piece = shifted(kt[n * 8 : n * 8 + 8, :], k * st)
                    tile = piece if tile is None else tile + piece
            corebuf[step, me, group * 8 : group * 8 + 8, :] = tile
        share(3 + 2 * step, corebuf.at[step])
        bytes_of(3 + 2 * step, corebuf.at[step], D).wait_recv()
        summed = -2.0 * jnp.sum(corebuf[step], axis=0)
        turned = jnp.concatenate(
            [
                lanes_below(shifted(summed[n // per * 8 : n // per * 8 + 8, :], -(n % per) * st), st)
                for n in range(st // 8)
            ],
            axis=0,
        )
    u_out[...] = urow[pl.ds(s * nr, nr), :] * UNIT
    square[:st, :] = turned
    core_out[...] = square[...].T[:rank, :rank]

    bytes_of(last, gbuf, S).wait_recv()
    g_out[...] = gbuf[...]
    bytes_of(0, srcbuf, D).wait_send()
    bytes_of(1, tgtbuf, S).wait_send()
    bytes_of(last, gbuf, S).wait_send()
    for step in range(OUTER):
        bytes_of(2 + 2 * step, lsebuf.at[step], D).wait_send()
        bytes_of(3 + 2 * step, corebuf.at[step], D).wait_send()


def place(*refs):
    count = (len(refs) - 1) // 2
    copies = [pltpu.make_async_copy(refs[k], refs[count + k], refs[-1].at[k]) for k in range(count)]
    for copy in copies:
        copy.start()
    for copy in copies:
        copy.wait()


def shards(src_feat, tgt_feat, tgt_dual, core_matrix):
    S, T = lax.axis_size("src"), lax.axis_size("tgt")
    D = S * T
    rows, fs = src_feat.shape
    held, ft = tgt_feat.shape
    feat = fs * T
    cols = held // S
    ns, nt = rows * S, held * T
    rank = feat + 2
    st = -(-rank // 8) * 8
    jr, nr = cols // LANES, rows // LANES
    per = LANES // st
    groups = -(-(st // 8) // per)
    deep = -(-6 * st // LANES) * LANES
    wide = -(-3 * st // LANES) * LANES
    dims = (S, T, rows, cols, fs, ft, feat, ns, nt)
    src = src_feat.T
    tgt = tgt_feat.reshape(S * jr, LANES, ft).transpose(0, 2, 1).reshape(S, jr * ft, LANES)
    dual = tgt_dual.reshape(S, jr, LANES)
    phases = 2 + 2 * OUTER + 1
    vmem = pl.BlockSpec(memory_space=pltpu.VMEM)
    u, g, core = pl.pallas_call(
        functools.partial(kernel, dims),
        out_shape=(
            jax.ShapeDtypeStruct((nr, LANES), F32),
            jax.ShapeDtypeStruct((S, jr, LANES), F32),
            jax.ShapeDtypeStruct((rank, rank), F32),
        ),
        in_specs=[pl.BlockSpec(memory_space=pltpu.HBM)] * 4,
        out_specs=(vmem,) * 3,
        scratch_shapes=[
            pltpu.VMEM((D, fs, rows), F32),
            pltpu.VMEM((S, jr * ft, LANES), F32),
            pltpu.VMEM((S, jr * ft, LANES), F32),
            pltpu.VMEM((jr, LANES), F32),
            pltpu.VMEM((rank, rank), F32),
            pltpu.VMEM((OUTER, D, ns // LANES, LANES), F32),
            pltpu.VMEM((OUTER, D, groups * 8, LANES), F32),
            pltpu.VMEM((S, jr, LANES), F32),
            pltpu.VMEM((st, ns), F32),
            pltpu.VMEM((st, ns), F32),
            pltpu.VMEM((st, cols), F32),
            pltpu.VMEM((st, cols), F32),
            pltpu.VMEM((wide, ns), BF16),
            pltpu.VMEM((ns, wide), BF16),
            pltpu.VMEM((wide, cols), BF16),
            pltpu.VMEM((cols, deep), BF16),
            pltpu.VMEM((deep, ns), BF16),
            pltpu.VMEM((cols, ns), F32),
            pltpu.VMEM((cols, LANES), F32),
            pltpu.VMEM((cols, 2 * wide), BF16),
            pltpu.VMEM((ns // LANES, LANES), F32),
            pltpu.VMEM((LANES, LANES), F32),
            pltpu.SemaphoreType.DMA((phases,)),
            pltpu.SemaphoreType.DMA((phases,)),
            pltpu.SemaphoreType.DMA((4,)),
        ],
        compiler_params=pltpu.CompilerParams(
            collective_id=0, has_side_effects=True, vmem_limit_bytes=64 * 1024 * 1024
        ),
    )(src, tgt, dual, core_matrix)
    placed = [u, g, core]
    u, g, core = pl.pallas_call(
        place,
        out_shape=[jax.ShapeDtypeStruct(x.shape, x.dtype) for x in placed],
        in_specs=[pl.BlockSpec(memory_space=pltpu.HBM)] * 3,
        out_specs=[pl.BlockSpec(memory_space=pltpu.HBM)] * 3,
        scratch_shapes=[pltpu.SemaphoreType.DMA((3,))],
        compiler_params=pltpu.CompilerParams(vmem_limit_bytes=64 * 1024 * 1024),
    )(*placed)
    return u.reshape(rows), g.reshape(held), core


def solution(mesh):
    placed = (
        P(("pairs", "src"), "tgt"),
        P(("pairs", "tgt"), "src"),
        P(("pairs", "tgt")),
        P("pairs", None),
    )
    return jax.shard_map(
        shards,
        mesh=mesh,
        in_specs=placed,
        out_specs=(P(("pairs", "src")), P(("pairs", "tgt")), P("pairs", None)),
        check_vma=False,
    )
```

```python
import functools
import math

import jax
import jax.numpy as jnp
from jax import lax
from jax.experimental import pallas as pl
from jax.experimental.pallas import tpu as pltpu
from jax.sharding import PartitionSpec as P

OUTER = 2
EPSILON = 0.02
LOG2E = math.log2(math.e)
UNIT = EPSILON / LOG2E
LANES = 128
MESH = pl.DeviceIdType.MESH
BF16 = jnp.bfloat16
F32 = jnp.float32


def split3(x):
    high = x.astype(BF16).astype(F32)
    rest = x - high
    mid = rest.astype(BF16).astype(F32)
    return high, mid, rest - mid


def lanes_below(x, count):
    return jnp.where(lax.broadcasted_iota(jnp.int32, x.shape, 1) < count, x, 0.0)


def shifted(x, by):
    return x if by % LANES == 0 else pltpu.roll(x, by % LANES, 1)


def kernel(
    dims, src_ref, tgt_ref, dual_ref, core_ref, u_out, g_out, core_out,
    srcbuf, tgtall, tgtbuf, dualbuf, corein, lsebuf, corebuf, gbuf, sl, sr, tl, tr, sls, srs, tls, trt, sps, logits, gcol, weighted, ehigh, elow, urow, square,
    send_sem, recv_sem, local_sem,
):
    S, T, rows, cols, fs, ft, feat, ns, nt = dims
    D = S * T
    rank = feat + 2
    st = -(-rank // 8) * 8
    jr = cols // LANES
    nr = rows // LANES
    last = 2 + 2 * OUTER
    s, t = lax.axis_index("src"), lax.axis_index("tgt")
    me = s * T + t

    def everyone(act):
        def body(k, unused):
            ps = lax.rem(s + k, S)
            for h in range(T):
                pt = lax.rem(t + h, T)
                act(ps, pt)
            return unused

        lax.fori_loop(1, S, body, 0, unroll=S <= 8)
        for h in range(1, T):
            act(s, lax.rem(t + h, T))

    def column(act):
        def body(k, unused):
            act(lax.rem(s + k, S))
            return unused

        lax.fori_loop(1, S, body, 0, unroll=S <= 8)

    def remote(phase, src, dst, device):
        return pltpu.make_async_remote_copy(
            src_ref=src, dst_ref=dst, send_sem=send_sem.at[phase], recv_sem=recv_sem.at[phase],
            device_id=device, device_id_type=MESH,
        )

    def share(phase, slots):
        def act(ps, pt):
            remote(phase, slots.at[me], slots.at[me], {"src": ps, "tgt": pt}).start()

        everyone(act)

    def bytes_of(phase, slots, count):
        part = slots.at[pl.ds(0, count - 1)]
        return remote(phase, part, part, {"src": lax.rem(s + 1, S)})

    copies = [
        pltpu.make_async_copy(src_ref, srcbuf.at[me], local_sem.at[0]),
        pltpu.make_async_copy(tgt_ref, tgtall, local_sem.at[1]),
        pltpu.make_async_copy(dual_ref.at[s], dualbuf, local_sem.at[2]),
        pltpu.make_async_copy(core_ref, corein, local_sem.at[3]),
    ]
    for copy in copies:
        copy.start()
    barrier = pltpu.get_barrier_semaphore()

    def greet(ps, pt):
        pl.semaphore_signal(barrier, inc=1, device_id={"src": ps, "tgt": pt}, device_id_type=MESH)

    everyone(greet)
    for copy in copies:
        copy.wait()
    tgtbuf[s] = tgtall[s]
    own_dual = dualbuf[...] * (1.0 / UNIT)
    for r in range(jr):
        gcol[r * LANES : (r + 1) * LANES, :] = jnp.broadcast_to(own_dual[r : r + 1, :], (LANES, LANES)).T
    square[...] = jnp.zeros_like(square)
    square[:rank, :rank] = corein[...]
    turned = square[...].T[:st, :]
    pl.semaphore_wait(barrier, D - 1)

    def send_tgt(ps):
        remote(1, tgtall.at[ps], tgtbuf.at[s], {"src": ps}).start()

    column(send_tgt)

    def send_src(ps, pt):
        remote(0, srcbuf.at[me], srcbuf.at[me], {"src": ps, "tgt": pt}).start()

    everyone(send_src)
    bytes_of(1, tgtbuf, S).wait_recv()

    def lift(ref, values, ahead, scale):
        ref[rank:, :] = jnp.zeros_like(ref[rank:, :])
        squares = jnp.sum(values * values, axis=0, keepdims=True)
        ones = jnp.ones_like(squares)
        ref[0:1, :] = squares if ahead else ones
        ref[1:2, :] = ones if ahead else squares
        ref[2:rank, :] = values if scale is None else scale * values

    def stacked(parts, height):
        width = parts[0].shape[1]
        fill = height - st * len(parts)
        return jnp.concatenate(list(parts) + ([jnp.zeros((fill, width), F32)] if fill else []), axis=0)

    deep = trt.shape[1]
    wide = srs.shape[1]
    for k in range(S):
        for r in range(jr):
            tr[2 + k * ft : 2 + (k + 1) * ft, r * LANES : (r + 1) * LANES] = tgtbuf[k, r * ft : (r + 1) * ft, :]
    lift(tr, tr[2:rank, :], False, None)
    t0, t1, t2 = split3(tr[...])
    trt[...] = stacked((t0, t1, t0, t1, t2, t0), deep).astype(BF16).T

    bytes_of(0, srcbuf, D).wait_recv()
    for k in range(S):
        for h in range(T):
            sr[2 + h * fs : 2 + (h + 1) * fs, k * rows : (k + 1) * rows] = srcbuf[k * T + h]
    lift(sl, sr[2:rank, :], True, -2.0)
    sls[...] = stacked(split3(sl[...]), wide).astype(BF16)

    per = LANES // st
    block = min(256, ns)
    chunk = min(256, cols)
    for step in range(OUTER):
        k0, k1, k2 = split3(turned * (-1.0 / UNIT))
        lhs = stacked(
            (k0 + shifted(k0, st) + shifted(k0, 2 * st), k1 + shifted(k1, st), k2), 3 * st
        ).astype(BF16)
        proj = jnp.dot(lhs, sls[...], preferred_element_type=F32)
        proj = proj[:st] + (proj[st : 2 * st] + proj[2 * st :])
        p0, p1, p2 = split3(proj)
        sps[...] = stacked((p0, p0, p1, p1, p0, p2), deep).astype(BF16)
        for b in range(ns // block):
            part = jnp.dot(trt[...], sps[:, b * block : (b + 1) * block], preferred_element_type=F32)
            for h in range(block // LANES):
                at = b * block // LANES + h
                tops, totals = [], []
                for c in range(cols // chunk):
                    rows_c = slice(c * chunk, (c + 1) * chunk)
                    here = part[rows_c, h * LANES : (h + 1) * LANES] + gcol[rows_c, :]
                    logits[rows_c, at * LANES : (at + 1) * LANES] = here
                    top = jnp.max(here, axis=0, keepdims=True)
                    tops.append(top)
                    totals.append(jnp.sum(jnp.exp2(here - top), axis=0, keepdims=True))
                top = functools.reduce(jnp.maximum, tops)
                total = sum(x * jnp.exp2(y - top) for x, y in zip(totals, tops))
                lsebuf[step, me, at : at + 1, :] = top + jnp.log2(total)
        share(2 + 2 * step, lsebuf.at[step])
        if step == 0:
            lift(tl, tr[2:rank, :], True, -2.0)
            tls[...] = stacked(split3(tl[...]), wide).astype(BF16)
            lift(sr, sr[2:rank, :], False, None)
            srs[...] = stacked(split3(sr[...]), wide).astype(BF16).T
        bytes_of(2 + 2 * step, lsebuf.at[step], D).wait_recv()
        top = jnp.max(lsebuf[step], axis=0)
        total = jnp.sum(jnp.exp2(lsebuf[step] - top[None]), axis=0)
        urow[...] = -math.log2(ns) - (top + jnp.log2(total))
        u_all = jnp.concatenate([urow[k : k + 1, :] for k in range(ns // LANES)], axis=1)
        for c in range(cols // chunk):
            sl_c = slice(c * chunk, (c + 1) * chunk)
            tops = []
            for k in range(chunk // 16):
                x = logits[c * chunk + k * 16 : c * chunk + (k + 1) * 16, :] + u_all
                top = jnp.max(x, axis=1, keepdims=True)
                e = jnp.exp2(x - top)
                high = e.astype(BF16)
                ehigh[c, k * 16 : (k + 1) * 16, :] = high
                elow[c, k * 16 : (k + 1) * 16, :] = (e - high.astype(F32)).astype(BF16)
                tops.append(top)
            top = jnp.concatenate(tops, axis=0)
            acc = jnp.dot(ehigh[c], srs[...], preferred_element_type=F32) + jnp.dot(elow[c], srs[...], preferred_element_type=F32)
            total = acc[:, 0:1]
            scaled = acc * (1.0 / total)
            first = scaled.astype(BF16)
            weighted[sl_c, :wide] = first
            weighted[sl_c, wide:] = (scaled - first.astype(F32)).astype(BF16)
            gcol[sl_c, :] = (gcol[sl_c, :] - math.log2(nt)) - (top + jnp.log2(total))
        ext = jnp.dot(tls[...], weighted[...], preferred_element_type=F32)
        ext = ext[:, :wide] + ext[:, wide:]
        kt = ext[:st] + (ext[st : 2 * st] + ext[2 * st : 3 * st])
        kt = kt + (shifted(kt, -st) + shifted(kt, -2 * st))
        kt = lanes_below(kt * (1.0 / nt), st)
        for group in range(corebuf.shape[2] // 8):
            tile = None
            for k in range(per):
                n = group * per + k
                if n * 8 < st:
                    piece = shifted(kt[n * 8 : n * 8 + 8, :], k * st)
                    tile = piece if tile is None else tile + piece
            corebuf[step, me, group * 8 : group * 8 + 8, :] = tile
        share(3 + 2 * step, corebuf.at[step])
        if step == OUTER - 1:
            for r in range(jr):
                gbuf[s, r : r + 1, :] = gcol[r * LANES : (r + 1) * LANES, :].T[0:1, :] * UNIT

            def send_g(ps):
                remote(last, gbuf.at[s], gbuf.at[s], {"src": ps}).start()

            column(send_g)
        bytes_of(3 + 2 * step, corebuf.at[step], D).wait_recv()
        summed = -2.0 * jnp.sum(corebuf[step], axis=0)
        turned = jnp.concatenate(
            [
                lanes_below(shifted(summed[n // per * 8 : n // per * 8 + 8, :], -(n % per) * st), st)
                for n in range(st // 8)
            ],
            axis=0,
        )
    u_out[...] = urow[pl.ds(s * nr, nr), :] * UNIT
    square[:st, :] = turned
    core_out[...] = square[...].T[:rank, :rank]

    bytes_of(last, gbuf, S).wait_recv()
    g_out[...] = gbuf[...]
    bytes_of(0, srcbuf, D).wait_send()
    bytes_of(1, tgtbuf, S).wait_send()
    bytes_of(last, gbuf, S).wait_send()
    for step in range(OUTER):
        bytes_of(2 + 2 * step, lsebuf.at[step], D).wait_send()
        bytes_of(3 + 2 * step, corebuf.at[step], D).wait_send()


def shards(src_feat, tgt_feat, tgt_dual, core_matrix):
    S, T = lax.axis_size("src"), lax.axis_size("tgt")
    D = S * T
    rows, fs = src_feat.shape
    held, ft = tgt_feat.shape
    feat = fs * T
    cols = held // S
    ns, nt = rows * S, held * T
    rank = feat + 2
    st = -(-rank // 8) * 8
    jr, nr = cols // LANES, rows // LANES
    per = LANES // st
    groups = -(-(st // 8) // per)
    deep = -(-6 * st // LANES) * LANES
    wide = -(-3 * st // LANES) * LANES
    dims = (S, T, rows, cols, fs, ft, feat, ns, nt)
    chunk = min(256, cols)
    src = src_feat.T
    tgt = tgt_feat.reshape(S * jr, LANES, ft).transpose(0, 2, 1).reshape(S, jr * ft, LANES)
    dual = tgt_dual.reshape(S, jr, LANES)
    phases = 2 + 2 * OUTER + 1
    vmem = pl.BlockSpec(memory_space=pltpu.VMEM)
    u, g, core = pl.pallas_call(
        functools.partial(kernel, dims),
        out_shape=(
            jax.ShapeDtypeStruct((nr, LANES), F32),
            jax.ShapeDtypeStruct((S, jr, LANES), F32),
            jax.ShapeDtypeStruct((rank, rank), F32),
        ),
        in_specs=[pl.BlockSpec(memory_space=pltpu.HBM)] * 4,
        out_specs=(vmem,) * 3,
        scratch_shapes=[
            pltpu.VMEM((D, fs, rows), F32),
            pltpu.VMEM((S, jr * ft, LANES), F32),
            pltpu.VMEM((S, jr * ft, LANES), F32),
            pltpu.VMEM((jr, LANES), F32),
            pltpu.VMEM((rank, rank), F32),
            pltpu.VMEM((OUTER, D, ns // LANES, LANES), F32),
            pltpu.VMEM((OUTER, D, groups * 8, LANES), F32),
            pltpu.VMEM((S, jr, LANES), F32),
            pltpu.VMEM((st, ns), F32),
            pltpu.VMEM((st, ns), F32),
            pltpu.VMEM((st, cols), F32),
            pltpu.VMEM((st, cols), F32),
            pltpu.VMEM((wide, ns), BF16),
            pltpu.VMEM((ns, wide), BF16),
            pltpu.VMEM((wide, cols), BF16),
            pltpu.VMEM((cols, deep), BF16),
            pltpu.VMEM((deep, ns), BF16),
            pltpu.VMEM((cols, ns), F32),
            pltpu.VMEM((cols, LANES), F32),
            pltpu.VMEM((cols, 2 * wide), BF16),
            pltpu.VMEM((cols // chunk, chunk, ns), BF16),
            pltpu.VMEM((cols // chunk, chunk, ns), BF16),
            pltpu.VMEM((ns // LANES, LANES), F32),
            pltpu.VMEM((LANES, LANES), F32),
            pltpu.SemaphoreType.DMA((phases,)),
            pltpu.SemaphoreType.DMA((phases,)),
            pltpu.SemaphoreType.DMA((4,)),
        ],
        compiler_params=pltpu.CompilerParams(
            collective_id=0, has_side_effects=True, vmem_limit_bytes=64 * 1024 * 1024
        ),
    )(src, tgt, dual, core_matrix)
    return u.reshape(rows), g.reshape(held), core


def solution(mesh):
    placed = (
        P(("pairs", "src"), "tgt"),
        P(("pairs", "tgt"), "src"),
        P(("pairs", "tgt")),
        P("pairs", None),
    )
    return jax.shard_map(
        shards,
        mesh=mesh,
        in_specs=placed,
        out_specs=(P(("pairs", "src")), P(("pairs", "tgt")), P("pairs", None)),
        check_vma=False,
    )
```

```python
import functools
import math

import jax
import jax.numpy as jnp
from jax import lax
from jax.experimental import pallas as pl
from jax.experimental.pallas import tpu as pltpu
from jax.sharding import PartitionSpec as P

OUTER = 2
EPSILON = 0.02
LOG2E = math.log2(math.e)
UNIT = EPSILON / LOG2E
LANES = 128
MESH = pl.DeviceIdType.MESH
BF16 = jnp.bfloat16
F32 = jnp.float32


def split3(x):
    high = x.astype(BF16).astype(F32)
    rest = x - high
    mid = rest.astype(BF16).astype(F32)
    return high, mid, rest - mid


def joined(logs):
    top = jnp.max(logs, axis=0)
    return top + jnp.log2(jnp.sum(jnp.exp2(logs - top[None]), axis=0))


def lanes_below(x, count):
    return jnp.where(lax.broadcasted_iota(jnp.int32, x.shape, 1) < count, x, 0.0)


def shifted(x, by):
    return x if by % LANES == 0 else pltpu.roll(x, by % LANES, 1)


def kernel(
    dims, src_ref, tgt_ref, dual_ref, core_ref, u_out, g_out, core_out,
    srcbuf, tgtall, tgtbuf, dualbuf, corein, lsepair, lsebuf, corepair, corebuf, gbuf, sl, sr, tl, tr, sls, srs, tls, trt, sps, logits, gcol, weighted, ehigh, elow, urow, square,
    send_sem, recv_sem, local_sem,
):
    S, T, rows, cols, fs, ft, feat, ns, nt = dims
    rank = feat + 2
    st = -(-rank // 8) * 8
    jr = cols // LANES
    nr = rows // LANES
    last = 3 + 4 * OUTER
    s, t = lax.axis_index("src"), lax.axis_index("tgt")

    def beside(act):
        for h in range(1, T):
            act(lax.rem(t + h, T))

    def column(act):
        def body(k, unused):
            act(lax.rem(s + k, S))
            return unused

        lax.fori_loop(1, S, body, 0, unroll=S <= 8)

    def remote(phase, src, dst, device):
        return pltpu.make_async_remote_copy(
            src_ref=src, dst_ref=dst, send_sem=send_sem.at[phase], recv_sem=recv_sem.at[phase],
            device_id=device, device_id_type=MESH,
        )

    def bytes_of(phase, slots, count):
        part = slots.at[pl.ds(0, count - 1)]
        return remote(phase, part, part, {"src": lax.rem(s + 1, S)})

    def over_tgt(phase, slots):
        beside(lambda pt: remote(phase, slots.at[t], slots.at[t], {"tgt": pt}).start())

    def over_src(phase, slots):
        column(lambda ps: remote(phase, slots.at[s], slots.at[s], {"src": ps}).start())

    copies = [
        pltpu.make_async_copy(src_ref, srcbuf.at[t, s], local_sem.at[0]),
        pltpu.make_async_copy(tgt_ref, tgtall, local_sem.at[1]),
        pltpu.make_async_copy(dual_ref.at[s], dualbuf, local_sem.at[2]),
        pltpu.make_async_copy(core_ref, corein, local_sem.at[3]),
    ]
    for copy in copies:
        copy.start()
    barrier = pltpu.get_barrier_semaphore()

    def greet(device):
        pl.semaphore_signal(barrier, inc=1, device_id=device, device_id_type=MESH)

    column(lambda ps: greet({"src": ps}))
    beside(lambda pt: greet({"tgt": pt}))
    for copy in copies:
        copy.wait()
    tgtbuf[s] = tgtall[s]
    own_dual = dualbuf[...] * (1.0 / UNIT)
    for r in range(jr):
        gcol[r * LANES : (r + 1) * LANES, :] = jnp.broadcast_to(own_dual[r : r + 1, :], (LANES, LANES)).T
    square[...] = jnp.zeros_like(square)
    square[:rank, :rank] = corein[...]
    turned = square[...].T[:st, :]
    pl.semaphore_wait(barrier, S + T - 2)

    over_src(0, srcbuf.at[t])
    column(lambda ps: remote(1, tgtall.at[ps], tgtbuf.at[s], {"src": ps}).start())
    bytes_of(0, srcbuf.at[t], S).wait_recv()
    over_tgt(2, srcbuf)
    bytes_of(1, tgtbuf, S).wait_recv()

    def lift(ref, values, ahead, scale):
        ref[rank:, :] = jnp.zeros_like(ref[rank:, :])
        squares = jnp.sum(values * values, axis=0, keepdims=True)
        ones = jnp.ones_like(squares)
        ref[0:1, :] = squares if ahead else ones
        ref[1:2, :] = ones if ahead else squares
        ref[2:rank, :] = values if scale is None else scale * values

    def stacked(parts, height):
        width = parts[0].shape[1]
        fill = height - st * len(parts)
        return jnp.concatenate(list(parts) + ([jnp.zeros((fill, width), F32)] if fill else []), axis=0)

    deep = trt.shape[1]
    wide = srs.shape[1]
    for k in range(S):
        for r in range(jr):
            tr[2 + k * ft : 2 + (k + 1) * ft, r * LANES : (r + 1) * LANES] = tgtbuf[k, r * ft : (r + 1) * ft, :]
    lift(tr, tr[2:rank, :], False, None)
    t0, t1, t2 = split3(tr[...])
    trt[...] = stacked((t0, t1, t0, t1, t2, t0), deep).astype(BF16).T

    bytes_of(2, srcbuf, T).wait_recv()
    for k in range(S):
        for h in range(T):
            sr[2 + h * fs : 2 + (h + 1) * fs, k * rows : (k + 1) * rows] = srcbuf[h, k]
    lift(sl, sr[2:rank, :], True, -2.0)
    sls[...] = stacked(split3(sl[...]), wide).astype(BF16)

    per = LANES // st
    block = min(256, ns)
    chunk = min(256, cols)
    for step in range(OUTER):
        k0, k1, k2 = split3(turned * (-1.0 / UNIT))
        lhs = stacked(
            (k0 + shifted(k0, st) + shifted(k0, 2 * st), k1 + shifted(k1, st), k2), 3 * st
        ).astype(BF16)
        proj = jnp.dot(lhs, sls[...], preferred_element_type=F32)
        proj = proj[:st] + (proj[st : 2 * st] + proj[2 * st :])
        p0, p1, p2 = split3(proj)
        sps[...] = stacked((p0, p0, p1, p1, p0, p2), deep).astype(BF16)
        for b in range(ns // block):
            part = jnp.dot(trt[...], sps[:, b * block : (b + 1) * block], preferred_element_type=F32)
            for h in range(block // LANES):
                at = b * block // LANES + h
                tops, totals = [], []
                for c in range(cols // chunk):
                    rows_c = slice(c * chunk, (c + 1) * chunk)
                    here = part[rows_c, h * LANES : (h + 1) * LANES] + gcol[rows_c, :]
                    logits[rows_c, at * LANES : (at + 1) * LANES] = here
                    top = jnp.max(here, axis=0, keepdims=True)
                    tops.append(top)
                    totals.append(jnp.sum(jnp.exp2(here - top), axis=0, keepdims=True))
                top = functools.reduce(jnp.maximum, tops)
                total = sum(x * jnp.exp2(y - top) for x, y in zip(totals, tops))
                lsepair[step, t, at : at + 1, :] = top + jnp.log2(total)
        phase = 3 + 4 * step
        over_tgt(phase, lsepair.at[step])
        bytes_of(phase, lsepair.at[step], T).wait_recv()
        lsebuf[step, s] = joined(lsepair[step])
        over_src(phase + 1, lsebuf.at[step])
        if step == 0:
            lift(tl, tr[2:rank, :], True, -2.0)
            tls[...] = stacked(split3(tl[...]), wide).astype(BF16)
            lift(sr, sr[2:rank, :], False, None)
            srs[...] = stacked(split3(sr[...]), wide).astype(BF16).T
        bytes_of(phase + 1, lsebuf.at[step], S).wait_recv()
        urow[...] = -math.log2(ns) - joined(lsebuf[step])
        u_all = jnp.concatenate([urow[k : k + 1, :] for k in range(ns // LANES)], axis=1)
        for c in range(cols // chunk):
            sl_c = slice(c * chunk, (c + 1) * chunk)
            tops = []
            for k in range(chunk // 16):
                x = logits[c * chunk + k * 16 : c * chunk + (k + 1) * 16, :] + u_all
                top = jnp.max(x, axis=1, keepdims=True)
                e = jnp.exp2(x - top)
                high = e.astype(BF16)
                ehigh[c, k * 16 : (k + 1) * 16, :] = high
                elow[c, k * 16 : (k + 1) * 16, :] = (e - high.astype(F32)).astype(BF16)
                tops.append(top)
            top = jnp.concatenate(tops, axis=0)
            acc = jnp.dot(ehigh[c], srs[...], preferred_element_type=F32) + jnp.dot(elow[c], srs[...], preferred_element_type=F32)
            total = acc[:, 0:1]
            scaled = acc * (1.0 / total)
            first = scaled.astype(BF16)
            weighted[sl_c, :wide] = first
            weighted[sl_c, wide:] = (scaled - first.astype(F32)).astype(BF16)
            gcol[sl_c, :] = (gcol[sl_c, :] - math.log2(nt)) - (top + jnp.log2(total))
        ext = jnp.dot(tls[...], weighted[...], preferred_element_type=F32)
        ext = ext[:, :wide] + ext[:, wide:]
        kt = ext[:st] + (ext[st : 2 * st] + ext[2 * st : 3 * st])
        kt = kt + (shifted(kt, -st) + shifted(kt, -2 * st))
        kt = lanes_below(kt * (1.0 / nt), st)
        for group in range(corebuf.shape[2] // 8):
            tile = None
            for k in range(per):
                n = group * per + k
                if n * 8 < st:
                    piece = shifted(kt[n * 8 : n * 8 + 8, :], k * st)
                    tile = piece if tile is None else tile + piece
            corepair[step, t, group * 8 : group * 8 + 8, :] = tile
        over_tgt(phase + 2, corepair.at[step])
        bytes_of(phase + 2, corepair.at[step], T).wait_recv()
        corebuf[step, s] = jnp.sum(corepair[step], axis=0)
        over_src(phase + 3, corebuf.at[step])
        if step == OUTER - 1:
            for r in range(jr):
                gbuf[s, r : r + 1, :] = gcol[r * LANES : (r + 1) * LANES, :].T[0:1, :] * UNIT
            over_src(last, gbuf)
        bytes_of(phase + 3, corebuf.at[step], S).wait_recv()
        summed = -2.0 * jnp.sum(corebuf[step], axis=0)
        turned = jnp.concatenate(
            [
                lanes_below(shifted(summed[n // per * 8 : n // per * 8 + 8, :], -(n % per) * st), st)
                for n in range(st // 8)
            ],
            axis=0,
        )
    u_out[...] = urow[pl.ds(s * nr, nr), :] * UNIT
    square[:st, :] = turned
    core_out[...] = square[...].T[:rank, :rank]

    bytes_of(last, gbuf, S).wait_recv()
    g_out[...] = gbuf[...]
    bytes_of(0, srcbuf.at[t], S).wait_send()
    bytes_of(1, tgtbuf, S).wait_send()
    bytes_of(2, srcbuf, T).wait_send()
    for step in range(OUTER):
        phase = 3 + 4 * step
        bytes_of(phase, lsepair.at[step], T).wait_send()
        bytes_of(phase + 1, lsebuf.at[step], S).wait_send()
        bytes_of(phase + 2, corepair.at[step], T).wait_send()
        bytes_of(phase + 3, corebuf.at[step], S).wait_send()
    bytes_of(last, gbuf, S).wait_send()


def place(*refs):
    count = len(refs) // 2
    for k in range(count):
        refs[count + k][...] = refs[k][...]


def shards(src_feat, tgt_feat, tgt_dual, core_matrix):
    S, T = lax.axis_size("src"), lax.axis_size("tgt")
    rows, fs = src_feat.shape
    held, ft = tgt_feat.shape
    feat = fs * T
    cols = held // S
    ns, nt = rows * S, held * T
    rank = feat + 2
    st = -(-rank // 8) * 8
    jr, nr = cols // LANES, rows // LANES
    per = LANES // st
    groups = -(-(st // 8) // per)
    deep = -(-6 * st // LANES) * LANES
    wide = -(-3 * st // LANES) * LANES
    dims = (S, T, rows, cols, fs, ft, feat, ns, nt)
    chunk = min(256, cols)
    src = src_feat.T
    tgt = tgt_feat.reshape(S * jr, LANES, ft).transpose(0, 2, 1).reshape(S, jr * ft, LANES)
    dual = tgt_dual.reshape(S, jr, LANES)
    phases = 4 + 4 * OUTER
    vmem = pl.BlockSpec(memory_space=pltpu.VMEM)
    u, g, core = pl.pallas_call(
        functools.partial(kernel, dims),
        out_shape=(
            jax.ShapeDtypeStruct((nr, LANES), F32),
            jax.ShapeDtypeStruct((S, jr, LANES), F32),
            jax.ShapeDtypeStruct((rank, rank), F32),
        ),
        in_specs=[pl.BlockSpec(memory_space=pltpu.HBM)] * 4,
        out_specs=(vmem,) * 3,
        scratch_shapes=[
            pltpu.VMEM((T, S, fs, rows), F32),
            pltpu.VMEM((S, jr * ft, LANES), F32),
            pltpu.VMEM((S, jr * ft, LANES), F32),
            pltpu.VMEM((jr, LANES), F32),
            pltpu.VMEM((rank, rank), F32),
            pltpu.VMEM((OUTER, T, ns // LANES, LANES), F32),
            pltpu.VMEM((OUTER, S, ns // LANES, LANES), F32),
            pltpu.VMEM((OUTER, T, groups * 8, LANES), F32),
            pltpu.VMEM((OUTER, S, groups * 8, LANES), F32),
            pltpu.VMEM((S, jr, LANES), F32),
            pltpu.VMEM((st, ns), F32),
            pltpu.VMEM((st, ns), F32),
            pltpu.VMEM((st, cols), F32),
            pltpu.VMEM((st, cols), F32),
            pltpu.VMEM((wide, ns), BF16),
            pltpu.VMEM((ns, wide), BF16),
            pltpu.VMEM((wide, cols), BF16),
            pltpu.VMEM((cols, deep), BF16),
            pltpu.VMEM((deep, ns), BF16),
            pltpu.VMEM((cols, ns), F32),
            pltpu.VMEM((cols, LANES), F32),
            pltpu.VMEM((cols, 2 * wide), BF16),
            pltpu.VMEM((cols // chunk, chunk, ns), BF16),
            pltpu.VMEM((cols // chunk, chunk, ns), BF16),
            pltpu.VMEM((ns // LANES, LANES), F32),
            pltpu.VMEM((LANES, LANES), F32),
            pltpu.SemaphoreType.DMA((phases,)),
            pltpu.SemaphoreType.DMA((phases,)),
            pltpu.SemaphoreType.DMA((4,)),
        ],
        compiler_params=pltpu.CompilerParams(
            collective_id=0, has_side_effects=True, vmem_limit_bytes=64 * 1024 * 1024
        ),
    )(src, tgt, dual, core_matrix)
    placed = [u, g, core]
    u, g, core = pl.pallas_call(
        place,
        out_shape=[jax.ShapeDtypeStruct(x.shape, x.dtype) for x in placed],
        in_specs=[vmem] * 3,
        out_specs=[vmem] * 3,
        compiler_params=pltpu.CompilerParams(vmem_limit_bytes=64 * 1024 * 1024),
    )(*placed)
    return u.reshape(rows), g.reshape(held), core


def solution(mesh):
    placed = (
        P(("pairs", "src"), "tgt"),
        P(("pairs", "tgt"), "src"),
        P(("pairs", "tgt")),
        P("pairs", None),
    )
    return jax.shard_map(
        shards,
        mesh=mesh,
        in_specs=placed,
        out_specs=(P(("pairs", "src")), P(("pairs", "tgt")), P("pairs", None)),
        check_vma=False,
    )
```

```python
import functools
import math

import jax
import jax.numpy as jnp
from jax import lax
from jax.experimental import pallas as pl
from jax.experimental.pallas import tpu as pltpu
from jax.sharding import PartitionSpec as P

OUTER = 2
EPSILON = 0.02
LOG2E = math.log2(math.e)
UNIT = EPSILON / LOG2E
LANES = 128
MESH = pl.DeviceIdType.MESH
BF16 = jnp.bfloat16
F32 = jnp.float32


def split3(x):
    high = x.astype(BF16).astype(F32)
    rest = x - high
    mid = rest.astype(BF16).astype(F32)
    return high, mid, rest - mid


def joined(logs):
    top = jnp.max(logs, axis=0)
    return top + jnp.log2(jnp.sum(jnp.exp2(logs - top[None]), axis=0))


def lanes_below(x, count):
    return jnp.where(lax.broadcasted_iota(jnp.int32, x.shape, 1) < count, x, 0.0)


def shifted(x, by):
    return x if by % LANES == 0 else pltpu.roll(x, by % LANES, 1)


def kernel(
    dims, src_ref, tgt_ref, dual_ref, core_ref, u_out, g_out, core_out,
    srcbuf, tgtall, tgtbuf, dualbuf, corein, lsepair, lsebuf, corepair, corebuf, gbuf, values, lifted, sls, srs, tls, trt, logits, gcol, weighted,
    ehigh, elow, urow, uall, turned, square,
    send_sem, recv_sem, local_sem,
):
    S, T, rows, cols, fs, ft, feat, ns, nt = dims
    rank = feat + 2
    st = -(-rank // 8) * 8
    jr = cols // LANES
    nr = rows // LANES
    last = 3 + 4 * OUTER
    s, t = lax.axis_index("src"), lax.axis_index("tgt")

    def beside(act):
        for h in range(1, T):
            act(lax.rem(t + h, T))

    def column(act):
        def body(k, unused):
            act(lax.rem(s + k, S))
            return unused

        lax.fori_loop(1, S, body, 0)

    def remote(phase, src, dst, device):
        return pltpu.make_async_remote_copy(
            src_ref=src, dst_ref=dst, send_sem=send_sem.at[phase], recv_sem=recv_sem.at[phase],
            device_id=device, device_id_type=MESH,
        )

    def bytes_of(phase, slots, count):
        part = slots.at[pl.ds(0, count - 1)]
        return remote(phase, part, part, {"src": lax.rem(s + 1, S)})

    def over_tgt(phase, slots):
        beside(lambda pt: remote(phase, slots.at[t], slots.at[t], {"tgt": pt}).start())

    def over_src(phase, slots):
        column(lambda ps: remote(phase, slots.at[s], slots.at[s], {"src": ps}).start())

    copies = [
        pltpu.make_async_copy(src_ref, srcbuf.at[t, s], local_sem.at[0]),
        pltpu.make_async_copy(tgt_ref, tgtall, local_sem.at[1]),
        pltpu.make_async_copy(dual_ref.at[s], dualbuf, local_sem.at[2]),
        pltpu.make_async_copy(core_ref, corein, local_sem.at[3]),
    ]
    for copy in copies:
        copy.start()
    barrier = pltpu.get_barrier_semaphore()

    def greet(device):
        pl.semaphore_signal(barrier, inc=1, device_id=device, device_id_type=MESH)

    column(lambda ps: greet({"src": ps}))
    beside(lambda pt: greet({"tgt": pt}))
    for copy in copies:
        copy.wait()
    tgtbuf[s] = tgtall[s]

    def spread_dual(r, unused):
        row = dualbuf[pl.ds(r, 1), :] * (1.0 / UNIT)
        gcol[pl.ds(pl.multiple_of(r * LANES, LANES), LANES), :] = jnp.broadcast_to(row, (LANES, LANES)).T
        return unused

    lax.fori_loop(0, jr, spread_dual, 0)
    square[...] = jnp.zeros_like(square)
    square[:rank, :rank] = corein[...]
    turned[...] = square[...].T[:st, :]
    pl.semaphore_wait(barrier, S + T - 2)

    over_src(0, srcbuf.at[t])
    column(lambda ps: remote(1, tgtall.at[ps], tgtbuf.at[s], {"src": ps}).start())
    bytes_of(0, srcbuf.at[t], S).wait_recv()
    over_tgt(2, srcbuf)
    bytes_of(1, tgtbuf, S).wait_recv()

    def lift(values, ahead, scale):
        squares = jnp.sum(values * values, axis=0, keepdims=True)
        ones = jnp.ones_like(squares)
        lifted[rank:, :] = jnp.zeros_like(lifted[rank:, :])
        lifted[0:1, :] = squares if ahead else ones
        lifted[1:2, :] = ones if ahead else squares
        lifted[2:rank, :] = values if scale is None else scale * values
        return split3(lifted[...])

    def stacked(parts, height):
        width = parts[0].shape[1]
        fill = height - st * len(parts)
        return jnp.concatenate(list(parts) + ([jnp.zeros((fill, width), F32)] if fill else []), axis=0)

    deep = trt.shape[1]
    wide = srs.shape[1]

    def take_tgt(r, unused):
        for k in range(S):
            values[k * ft : (k + 1) * ft, :] = tgtbuf[k, r]
        here = pl.ds(pl.multiple_of(r * LANES, LANES), LANES)
        t0, t1, t2 = lift(values[...], False, None)
        trt[here, :] = stacked((t0, t1, t0, t1, t2, t0), deep).astype(BF16).T
        tls[:, here] = stacked(lift(values[...], True, -2.0), wide).astype(BF16)
        return unused

    lax.fori_loop(0, jr, take_tgt, 0)
    bytes_of(2, srcbuf, T).wait_recv()

    def take_src(k, unused):
        for r in range(nr):
            for h in range(T):
                values[h * fs : (h + 1) * fs, :] = srcbuf[h, k, :, r * LANES : (r + 1) * LANES]
            here = pl.ds(pl.multiple_of((k * nr + r) * LANES, LANES), LANES)
            sls[:, here] = stacked(lift(values[...], True, -2.0), wide).astype(BF16)
            srs[here, :] = stacked(lift(values[...], False, None), wide).astype(BF16).T
        return unused

    lax.fori_loop(0, S, take_src, 0)
    per = LANES // st
    block = min(256, ns)
    chunk = min(256, cols)
    blocks = ns // block

    def outer(step, unused):
        phase = 3 + 4 * step
        k0, k1, k2 = split3(turned[...] * (-1.0 / UNIT))
        lhs = stacked(
            (k0 + shifted(k0, st) + shifted(k0, 2 * st), k1 + shifted(k1, st), k2), 3 * st
        ).astype(BF16)

        def row_block(b, unused):
            here_b = pl.ds(pl.multiple_of(b * block, LANES), block)
            proj = jnp.dot(lhs, sls[:, here_b], preferred_element_type=F32)
            proj = proj[:st] + (proj[st : 2 * st] + proj[2 * st :])
            p0, p1, p2 = split3(proj)
            sps = stacked((p0, p0, p1, p1, p0, p2), deep).astype(BF16)
            part = jnp.dot(trt[...], sps, preferred_element_type=F32)
            for h in range(block // LANES):
                lanes_h = slice(h * LANES, (h + 1) * LANES)
                tops, totals = [], []
                for c in range(cols // chunk):
                    rows_c = slice(c * chunk, (c + 1) * chunk)
                    here = part[rows_c, lanes_h] + gcol[rows_c, :]
                    logits[b, rows_c, lanes_h] = here
                    top = jnp.max(here, axis=0, keepdims=True)
                    tops.append(top)
                    totals.append(jnp.sum(jnp.exp2(here - top), axis=0, keepdims=True))
                top = functools.reduce(jnp.maximum, tops)
                total = sum(x * jnp.exp2(y - top) for x, y in zip(totals, tops))
                lsepair[step, t, pl.ds(b * (block // LANES) + h, 1), :] = top + jnp.log2(total)
            return unused

        lax.fori_loop(0, blocks, row_block, 0)
        over_tgt(phase, lsepair.at[step])
        bytes_of(phase, lsepair.at[step], T).wait_recv()
        lsebuf[step, s] = joined(lsepair[step])
        over_src(phase + 1, lsebuf.at[step])
        bytes_of(phase + 1, lsebuf.at[step], S).wait_recv()
        urow[...] = -math.log2(ns) - joined(lsebuf[step])
        for k in range(ns // LANES):
            uall[0:1, k * LANES : (k + 1) * LANES] = urow[k : k + 1, :]

        def col_chunk(c, unused):
            base = pl.multiple_of(c * chunk, chunk)

            def rows_of(k, unused):
                for n in range(4):
                    at = pl.multiple_of(k * 64 + n * 16, 16)
                    there = pl.ds(pl.multiple_of(base + at, 16), 16)
                    x = jnp.concatenate([logits[b, there, :] for b in range(blocks)], axis=1) + uall[0:1, :]
                    top = jnp.max(x, axis=1, keepdims=True)
                    e = jnp.exp2(x - top)
                    high = e.astype(BF16)
                    ehigh[pl.ds(at, 16), :] = high
                    elow[pl.ds(at, 16), :] = (e - high.astype(F32)).astype(BF16)
                    gcol[there, :] = gcol[there, :] - top
                return unused

            lax.fori_loop(0, chunk // 64, rows_of, 0)
            acc = jnp.dot(ehigh[...], srs[...], preferred_element_type=F32)
            acc = acc + jnp.dot(elow[...], srs[...], preferred_element_type=F32)
            total = acc[:, 0:1]
            scaled = acc * (1.0 / total)
            first = scaled.astype(BF16)
            here = pl.ds(base, chunk)
            weighted[here, :wide] = first
            weighted[here, wide:] = (scaled - first.astype(F32)).astype(BF16)
            gcol[here, :] = gcol[here, :] - (math.log2(nt) + jnp.log2(total))
            return unused

        lax.fori_loop(0, cols // chunk, col_chunk, 0)
        ext = jnp.dot(tls[...], weighted[...], preferred_element_type=F32)
        ext = ext[:, :wide] + ext[:, wide:]
        kt = ext[:st] + (ext[st : 2 * st] + ext[2 * st : 3 * st])
        kt = kt + (shifted(kt, -st) + shifted(kt, -2 * st))
        kt = lanes_below(kt * (1.0 / nt), st)
        for group in range(corebuf.shape[2] // 8):
            tile = None
            for k in range(per):
                n = group * per + k
                if n * 8 < st:
                    piece = shifted(kt[n * 8 : n * 8 + 8, :], k * st)
                    tile = piece if tile is None else tile + piece
            corepair[step, t, group * 8 : group * 8 + 8, :] = tile
        over_tgt(phase + 2, corepair.at[step])
        bytes_of(phase + 2, corepair.at[step], T).wait_recv()
        corebuf[step, s] = jnp.sum(corepair[step], axis=0)
        over_src(phase + 3, corebuf.at[step])

        @pl.when(step == OUTER - 1)
        def finish_dual():
            def lay(r, unused):
                piece = gcol[pl.ds(pl.multiple_of(r * LANES, LANES), LANES), :]
                gbuf[s, pl.ds(r, 1), :] = piece.T[0:1, :] * UNIT
                return unused

            lax.fori_loop(0, jr, lay, 0)
            over_src(last, gbuf)

        bytes_of(phase + 3, corebuf.at[step], S).wait_recv()
        summed = -2.0 * jnp.sum(corebuf[step], axis=0)
        turned[...] = jnp.concatenate(
            [
                lanes_below(shifted(summed[n // per * 8 : n // per * 8 + 8, :], -(n % per) * st), st)
                for n in range(st // 8)
            ],
            axis=0,
        )
        return unused

    lax.fori_loop(0, OUTER, outer, 0)
    u_out[...] = urow[pl.ds(s * nr, nr), :] * UNIT
    square[:st, :] = turned[...]
    core_out[...] = square[...].T[:rank, :rank]

    bytes_of(last, gbuf, S).wait_recv()
    g_out[...] = gbuf[...]
    bytes_of(0, srcbuf.at[t], S).wait_send()
    bytes_of(1, tgtbuf, S).wait_send()
    bytes_of(2, srcbuf, T).wait_send()
    for step in range(OUTER):
        phase = 3 + 4 * step
        bytes_of(phase, lsepair.at[step], T).wait_send()
        bytes_of(phase + 1, lsebuf.at[step], S).wait_send()
        bytes_of(phase + 2, corepair.at[step], T).wait_send()
        bytes_of(phase + 3, corebuf.at[step], S).wait_send()
    bytes_of(last, gbuf, S).wait_send()


def place(*refs):
    count = len(refs) // 2
    for k in range(count):
        refs[count + k][...] = refs[k][...]


def shards(src_feat, tgt_feat, tgt_dual, core_matrix):
    S, T = lax.axis_size("src"), lax.axis_size("tgt")
    rows, fs = src_feat.shape
    held, ft = tgt_feat.shape
    feat = fs * T
    cols = held // S
    ns, nt = rows * S, held * T
    rank = feat + 2
    st = -(-rank // 8) * 8
    jr, nr = cols // LANES, rows // LANES
    per = LANES // st
    groups = -(-(st // 8) // per)
    deep = -(-6 * st // LANES) * LANES
    wide = -(-3 * st // LANES) * LANES
    dims = (S, T, rows, cols, fs, ft, feat, ns, nt)
    chunk, block = min(256, cols), min(256, ns)
    src = src_feat.T
    tgt = tgt_feat.reshape(S * jr, LANES, ft).transpose(0, 2, 1).reshape(S, jr, ft, LANES)
    dual = tgt_dual.reshape(S, jr, LANES)
    phases = 4 + 4 * OUTER
    vmem = pl.BlockSpec(memory_space=pltpu.VMEM)
    u, g, core = pl.pallas_call(
        functools.partial(kernel, dims),
        out_shape=(
            jax.ShapeDtypeStruct((nr, LANES), F32),
            jax.ShapeDtypeStruct((S, jr, LANES), F32),
            jax.ShapeDtypeStruct((rank, rank), F32),
        ),
        in_specs=[pl.BlockSpec(memory_space=pltpu.HBM)] * 4,
        out_specs=(vmem,) * 3,
        scratch_shapes=[
            pltpu.VMEM((T, S, fs, rows), F32),
            pltpu.VMEM((S, jr, ft, LANES), F32),
            pltpu.VMEM((S, jr, ft, LANES), F32),
            pltpu.VMEM((jr, LANES), F32),
            pltpu.VMEM((rank, rank), F32),
            pltpu.VMEM((OUTER, T, ns // LANES, LANES), F32),
            pltpu.VMEM((OUTER, S, ns // LANES, LANES), F32),
            pltpu.VMEM((OUTER, T, groups * 8, LANES), F32),
            pltpu.VMEM((OUTER, S, groups * 8, LANES), F32),
            pltpu.VMEM((S, jr, LANES), F32),
            pltpu.VMEM((feat, LANES), F32),
            pltpu.VMEM((st, LANES), F32),
            pltpu.VMEM((wide, ns), BF16),
            pltpu.VMEM((ns, wide), BF16),
            pltpu.VMEM((wide, cols), BF16),
            pltpu.VMEM((cols, deep), BF16),
            pltpu.VMEM((ns // block, cols, block), F32),
            pltpu.VMEM((cols, LANES), F32),
            pltpu.VMEM((cols, 2 * wide), BF16),
            pltpu.VMEM((chunk, ns), BF16),
            pltpu.VMEM((chunk, ns), BF16),
            pltpu.VMEM((ns // LANES, LANES), F32),
            pltpu.VMEM((1, ns), F32),
            pltpu.VMEM((st, LANES), F32),
            pltpu.VMEM((LANES, LANES), F32),
            pltpu.SemaphoreType.DMA((phases,)),
            pltpu.SemaphoreType.DMA((phases,)),
            pltpu.SemaphoreType.DMA((4,)),
        ],
        compiler_params=pltpu.CompilerParams(
            collective_id=0, has_side_effects=True, vmem_limit_bytes=64 * 1024 * 1024
        ),
    )(src, tgt, dual, core_matrix)
    placed = [u, g, core]
    u, g, core = pl.pallas_call(
        place,
        out_shape=[jax.ShapeDtypeStruct(x.shape, x.dtype) for x in placed],
        in_specs=[vmem] * 3,
        out_specs=[vmem] * 3,
        compiler_params=pltpu.CompilerParams(vmem_limit_bytes=64 * 1024 * 1024),
    )(*placed)
    return u.reshape(rows), g.reshape(held), core


def solution(mesh):
    placed = (
        P(("pairs", "src"), "tgt"),
        P(("pairs", "tgt"), "src"),
        P(("pairs", "tgt")),
        P("pairs", None),
    )
    return jax.shard_map(
        shards,
        mesh=mesh,
        in_specs=placed,
        out_specs=(P(("pairs", "src")), P(("pairs", "tgt")), P("pairs", None)),
        check_vma=False,
    )
```

```python
import functools
import math

import jax
import jax.numpy as jnp
from jax import lax
from jax.experimental import pallas as pl
from jax.experimental.pallas import tpu as pltpu
from jax.sharding import PartitionSpec as P

OUTER = 2
EPSILON = 0.02
LOG2E = math.log2(math.e)
UNIT = EPSILON / LOG2E
LANES = 128
MESH = pl.DeviceIdType.MESH
BF16 = jnp.bfloat16
F32 = jnp.float32


def split3(x):
    high = x.astype(BF16).astype(F32)
    rest = x - high
    mid = rest.astype(BF16).astype(F32)
    return high, mid, rest - mid


def joined(logs):
    top = jnp.max(logs, axis=0)
    return top + jnp.log2(jnp.sum(jnp.exp2(logs - top[None]), axis=0))


def lanes_below(x, count):
    return jnp.where(lax.broadcasted_iota(jnp.int32, x.shape, 1) < count, x, 0.0)


def shifted(x, by):
    return x if by % LANES == 0 else pltpu.roll(x, by % LANES, 1)


def kernel(
    dims, src_ref, tgt_ref, dual_ref, core_ref, u_out, g_out, core_out,
    srcbuf, tgtall, tgtbuf, dualbuf, corein, lsepair, lsebuf, corepair, corebuf, gbuf, sl, sr, tl, tr, sls, srs, tls, trt, sps, logits, gcol, weighted, ehigh, elow, urow, turned, square,
    send_sem, recv_sem, local_sem,
):
    S, T, rows, cols, fs, ft, feat, ns, nt = dims
    rank = feat + 2
    st = -(-rank // 8) * 8
    jr = cols // LANES
    nr = rows // LANES
    last = 3 + 4 * OUTER
    s, t = lax.axis_index("src"), lax.axis_index("tgt")

    def beside(act):
        for h in range(1, T):
            act(lax.rem(t + h, T))

    def column(act):
        def body(k, unused):
            act(lax.rem(s + k, S))
            return unused

        lax.fori_loop(1, S, body, 0, unroll=S <= 8)

    def remote(phase, src, dst, device):
        return pltpu.make_async_remote_copy(
            src_ref=src, dst_ref=dst, send_sem=send_sem.at[phase], recv_sem=recv_sem.at[phase],
            device_id=device, device_id_type=MESH,
        )

    def bytes_of(phase, slots, count):
        part = slots.at[pl.ds(0, count - 1)]
        return remote(phase, part, part, {"src": lax.rem(s + 1, S)})

    def over_tgt(phase, slots):
        beside(lambda pt: remote(phase, slots.at[t], slots.at[t], {"tgt": pt}).start())

    def over_src(phase, slots):
        column(lambda ps: remote(phase, slots.at[s], slots.at[s], {"src": ps}).start())

    copies = [
        pltpu.make_async_copy(src_ref, srcbuf.at[t, s], local_sem.at[0]),
        pltpu.make_async_copy(tgt_ref, tgtall, local_sem.at[1]),
        pltpu.make_async_copy(dual_ref.at[s], dualbuf, local_sem.at[2]),
        pltpu.make_async_copy(core_ref, corein, local_sem.at[3]),
    ]
    for copy in copies:
        copy.start()
    barrier = pltpu.get_barrier_semaphore()

    def greet(device):
        pl.semaphore_signal(barrier, inc=1, device_id=device, device_id_type=MESH)

    column(lambda ps: greet({"src": ps}))
    beside(lambda pt: greet({"tgt": pt}))
    for copy in copies:
        copy.wait()
    tgtbuf[s] = tgtall[s]
    own_dual = dualbuf[...] * (1.0 / UNIT)
    for r in range(jr):
        gcol[r * LANES : (r + 1) * LANES, :] = jnp.broadcast_to(own_dual[r : r + 1, :], (LANES, LANES)).T
    square[...] = jnp.zeros_like(square)
    square[:rank, :rank] = corein[...]
    turned[...] = square[...].T[:st, :]
    pl.semaphore_wait(barrier, S + T - 2)

    over_src(0, srcbuf.at[t])
    column(lambda ps: remote(1, tgtall.at[ps], tgtbuf.at[s], {"src": ps}).start())
    bytes_of(0, srcbuf.at[t], S).wait_recv()
    over_tgt(2, srcbuf)
    bytes_of(1, tgtbuf, S).wait_recv()

    def lift(ref, values, ahead, scale):
        ref[rank:, :] = jnp.zeros_like(ref[rank:, :])
        squares = jnp.sum(values * values, axis=0, keepdims=True)
        ones = jnp.ones_like(squares)
        ref[0:1, :] = squares if ahead else ones
        ref[1:2, :] = ones if ahead else squares
        ref[2:rank, :] = values if scale is None else scale * values

    def stacked(parts, height):
        width = parts[0].shape[1]
        fill = height - st * len(parts)
        return jnp.concatenate(list(parts) + ([jnp.zeros((fill, width), F32)] if fill else []), axis=0)

    deep = trt.shape[1]
    wide = srs.shape[1]
    for k in range(S):
        for r in range(jr):
            tr[2 + k * ft : 2 + (k + 1) * ft, r * LANES : (r + 1) * LANES] = tgtbuf[k, r * ft : (r + 1) * ft, :]
    lift(tr, tr[2:rank, :], False, None)
    t0, t1, t2 = split3(tr[...])
    trt[...] = stacked((t0, t1, t0, t1, t2, t0), deep).astype(BF16).T

    bytes_of(2, srcbuf, T).wait_recv()
    for k in range(S):
        for h in range(T):
            sr[2 + h * fs : 2 + (h + 1) * fs, k * rows : (k + 1) * rows] = srcbuf[h, k]
    lift(sl, sr[2:rank, :], True, -2.0)
    sls[...] = stacked(split3(sl[...]), wide).astype(BF16)

    per = LANES // st
    block = min(256, ns)
    chunk = min(256, cols)
    def outer(step, unused):
        k0, k1, k2 = split3(turned[...] * (-1.0 / UNIT))
        lhs = stacked(
            (k0 + shifted(k0, st) + shifted(k0, 2 * st), k1 + shifted(k1, st), k2), 3 * st
        ).astype(BF16)
        proj = jnp.dot(lhs, sls[...], preferred_element_type=F32)
        proj = proj[:st] + (proj[st : 2 * st] + proj[2 * st :])
        p0, p1, p2 = split3(proj)
        sps[...] = stacked((p0, p0, p1, p1, p0, p2), deep).astype(BF16)
        sublogs = []
        for b in range(ns // block):
            part = jnp.dot(trt[...], sps[:, b * block : (b + 1) * block], preferred_element_type=F32)
            for h in range(block // LANES):
                at = b * block // LANES + h
                tops = []
                for c in range(cols // chunk):
                    rows_c = slice(c * chunk, (c + 1) * chunk)
                    here = part[rows_c, h * LANES : (h + 1) * LANES] + gcol[rows_c, :]
                    logits[rows_c, at * LANES : (at + 1) * LANES] = here
                    tops.append(jnp.max(here.reshape(chunk // 8, 8, LANES), axis=0))
                top = functools.reduce(jnp.maximum, tops)
                totals = []
                for c in range(cols // chunk):
                    here = logits[c * chunk : (c + 1) * chunk, at * LANES : (at + 1) * LANES]
                    totals.append(jnp.sum(jnp.exp2(here.reshape(chunk // 8, 8, LANES) - top[None]), axis=0))
                sublogs.append(top + jnp.log2(sum(totals)))
        for at in range(ns // LANES):
            top = jnp.max(sublogs[at], axis=0, keepdims=True)
            total = jnp.sum(jnp.exp2(sublogs[at] - top), axis=0, keepdims=True)
            lsepair[step, t, at : at + 1, :] = top + jnp.log2(total)
        phase = 3 + 4 * step
        over_tgt(phase, lsepair.at[step])
        bytes_of(phase, lsepair.at[step], T).wait_recv()
        lsebuf[step, s] = joined(lsepair[step])
        over_src(phase + 1, lsebuf.at[step])

        @pl.when(step == 0)
        def prepare():
            lift(tl, tr[2:rank, :], True, -2.0)
            tls[...] = stacked(split3(tl[...]), wide).astype(BF16)
            lift(sr, sr[2:rank, :], False, None)
            srs[...] = stacked(split3(sr[...]), wide).astype(BF16).T

        bytes_of(phase + 1, lsebuf.at[step], S).wait_recv()
        urow[...] = -math.log2(ns) - joined(lsebuf[step])
        u_all = jnp.concatenate([urow[k : k + 1, :] for k in range(ns // LANES)], axis=1)
        for c in range(cols // chunk):
            sl_c = slice(c * chunk, (c + 1) * chunk)
            starts = range(c * chunk, (c + 1) * chunk, 16)
            tops = [jnp.max(logits[k : k + 16, :] + u_all, axis=1, keepdims=True) for k in starts]
            for k, top in zip(starts, tops):
                e = jnp.exp2((logits[k : k + 16, :] + u_all) - top)
                high = e.astype(BF16)
                ehigh[c, k - c * chunk : k - c * chunk + 16, :] = high
                elow[c, k - c * chunk : k - c * chunk + 16, :] = (e - high.astype(F32)).astype(BF16)
            top = jnp.concatenate(tops, axis=0)
            acc = jnp.dot(ehigh[c], srs[...], preferred_element_type=F32) + jnp.dot(elow[c], srs[...], preferred_element_type=F32)
            total = acc[:, 0:1]
            scaled = acc * (1.0 / total)
            first = scaled.astype(BF16)
            weighted[sl_c, :wide] = first
            weighted[sl_c, wide:] = (scaled - first.astype(F32)).astype(BF16)
            gcol[sl_c, :] = (gcol[sl_c, :] - math.log2(nt)) - (top + jnp.log2(total))
        ext = jnp.dot(tls[...], weighted[...], preferred_element_type=F32)
        ext = ext[:, :wide] + ext[:, wide:]
        kt = ext[:st] + (ext[st : 2 * st] + ext[2 * st : 3 * st])
        kt = kt + (shifted(kt, -st) + shifted(kt, -2 * st))
        kt = lanes_below(kt * (1.0 / nt), st)
        for group in range(corebuf.shape[2] // 8):
            tile = None
            for k in range(per):
                n = group * per + k
                if n * 8 < st:
                    piece = shifted(kt[n * 8 : n * 8 + 8, :], k * st)
                    tile = piece if tile is None else tile + piece
            corepair[step, t, group * 8 : group * 8 + 8, :] = tile
        over_tgt(phase + 2, corepair.at[step])
        bytes_of(phase + 2, corepair.at[step], T).wait_recv()
        corebuf[step, s] = jnp.sum(corepair[step], axis=0)
        over_src(phase + 3, corebuf.at[step])

        @pl.when(step == OUTER - 1)
        def finish_dual():
            for r in range(jr):
                gbuf[s, r : r + 1, :] = gcol[r * LANES : (r + 1) * LANES, :].T[0:1, :] * UNIT
            over_src(last, gbuf)

        bytes_of(phase + 3, corebuf.at[step], S).wait_recv()
        summed = -2.0 * jnp.sum(corebuf[step], axis=0)
        turned[...] = jnp.concatenate(
            [
                lanes_below(shifted(summed[n // per * 8 : n // per * 8 + 8, :], -(n % per) * st), st)
                for n in range(st // 8)
            ],
            axis=0,
        )
        return unused

    lax.fori_loop(0, OUTER, outer, 0)
    u_out[...] = urow[pl.ds(s * nr, nr), :] * UNIT
    square[:st, :] = turned[...]
    core_out[...] = square[...].T[:rank, :rank]

    bytes_of(last, gbuf, S).wait_recv()
    g_out[...] = gbuf[...]
    bytes_of(0, srcbuf.at[t], S).wait_send()
    bytes_of(1, tgtbuf, S).wait_send()
    bytes_of(2, srcbuf, T).wait_send()
    for step in range(OUTER):
        phase = 3 + 4 * step
        bytes_of(phase, lsepair.at[step], T).wait_send()
        bytes_of(phase + 1, lsebuf.at[step], S).wait_send()
        bytes_of(phase + 2, corepair.at[step], T).wait_send()
        bytes_of(phase + 3, corebuf.at[step], S).wait_send()
    bytes_of(last, gbuf, S).wait_send()


def place(*refs):
    count = len(refs) // 2
    for k in range(count):
        refs[count + k][...] = refs[k][...]


def shards(src_feat, tgt_feat, tgt_dual, core_matrix):
    S, T = lax.axis_size("src"), lax.axis_size("tgt")
    rows, fs = src_feat.shape
    held, ft = tgt_feat.shape
    feat = fs * T
    cols = held // S
    ns, nt = rows * S, held * T
    rank = feat + 2
    st = -(-rank // 8) * 8
    jr, nr = cols // LANES, rows // LANES
    per = LANES // st
    groups = -(-(st // 8) // per)
    deep = -(-6 * st // LANES) * LANES
    wide = -(-3 * st // LANES) * LANES
    dims = (S, T, rows, cols, fs, ft, feat, ns, nt)
    chunk = min(256, cols)
    src = src_feat.T
    tgt = tgt_feat.reshape(S * jr, LANES, ft).transpose(0, 2, 1).reshape(S, jr * ft, LANES)
    dual = tgt_dual.reshape(S, jr, LANES)
    phases = 4 + 4 * OUTER
    vmem = pl.BlockSpec(memory_space=pltpu.VMEM)
    u, g, core = pl.pallas_call(
        functools.partial(kernel, dims),
        out_shape=(
            jax.ShapeDtypeStruct((nr, LANES), F32),
            jax.ShapeDtypeStruct((S, jr, LANES), F32),
            jax.ShapeDtypeStruct((rank, rank), F32),
        ),
        in_specs=[pl.BlockSpec(memory_space=pltpu.HBM)] * 4,
        out_specs=(vmem,) * 3,
        scratch_shapes=[
            pltpu.VMEM((T, S, fs, rows), F32),
            pltpu.VMEM((S, jr * ft, LANES), F32),
            pltpu.VMEM((S, jr * ft, LANES), F32),
            pltpu.VMEM((jr, LANES), F32),
            pltpu.VMEM((rank, rank), F32),
            pltpu.VMEM((OUTER, T, ns // LANES, LANES), F32),
            pltpu.VMEM((OUTER, S, ns // LANES, LANES), F32),
            pltpu.VMEM((OUTER, T, groups * 8, LANES), F32),
            pltpu.VMEM((OUTER, S, groups * 8, LANES), F32),
            pltpu.VMEM((S, jr, LANES), F32),
            pltpu.VMEM((st, ns), F32),
            pltpu.VMEM((st, ns), F32),
            pltpu.VMEM((st, cols), F32),
            pltpu.VMEM((st, cols), F32),
            pltpu.VMEM((wide, ns), BF16),
            pltpu.VMEM((ns, wide), BF16),
            pltpu.VMEM((wide, cols), BF16),
            pltpu.VMEM((cols, deep), BF16),
            pltpu.VMEM((deep, ns), BF16),
            pltpu.VMEM((cols, ns), F32),
            pltpu.VMEM((cols, LANES), F32),
            pltpu.VMEM((cols, 2 * wide), BF16),
            pltpu.VMEM((cols // chunk, chunk, ns), BF16),
            pltpu.VMEM((cols // chunk, chunk, ns), BF16),
            pltpu.VMEM((ns // LANES, LANES), F32),
            pltpu.VMEM((st, LANES), F32),
            pltpu.VMEM((LANES, LANES), F32),
            pltpu.SemaphoreType.DMA((phases,)),
            pltpu.SemaphoreType.DMA((phases,)),
            pltpu.SemaphoreType.DMA((4,)),
        ],
        compiler_params=pltpu.CompilerParams(
            collective_id=0, has_side_effects=True, vmem_limit_bytes=64 * 1024 * 1024
        ),
    )(src, tgt, dual, core_matrix)
    placed = [u, g, core]
    u, g, core = pl.pallas_call(
        place,
        out_shape=[jax.ShapeDtypeStruct(x.shape, x.dtype) for x in placed],
        in_specs=[vmem] * 3,
        out_specs=[vmem] * 3,
        compiler_params=pltpu.CompilerParams(vmem_limit_bytes=64 * 1024 * 1024),
    )(*placed)
    return u.reshape(rows), g.reshape(held), core


def solution(mesh):
    placed = (
        P(("pairs", "src"), "tgt"),
        P(("pairs", "tgt"), "src"),
        P(("pairs", "tgt")),
        P("pairs", None),
    )
    return jax.shard_map(
        shards,
        mesh=mesh,
        in_specs=placed,
        out_specs=(P(("pairs", "src")), P(("pairs", "tgt")), P("pairs", None)),
        check_vma=False,
    )
```

```python
import functools
import math

import jax
import jax.numpy as jnp
from jax import lax
from jax.experimental import pallas as pl
from jax.experimental.pallas import tpu as pltpu
from jax.sharding import PartitionSpec as P

OUTER = 2
EPSILON = 0.02
LOG2E = math.log2(math.e)
UNIT = EPSILON / LOG2E
LANES = 128
MESH = pl.DeviceIdType.MESH
BF16 = jnp.bfloat16
F32 = jnp.float32


def split3(x):
    high = x.astype(BF16).astype(F32)
    rest = x - high
    mid = rest.astype(BF16).astype(F32)
    return high, mid, rest - mid


def joined(logs):
    top = jnp.max(logs, axis=0)
    return top + jnp.log2(jnp.sum(jnp.exp2(logs - top[None]), axis=0))


def lanes_below(x, count):
    return jnp.where(lax.broadcasted_iota(jnp.int32, x.shape, 1) < count, x, 0.0)


def shifted(x, by):
    return x if by % LANES == 0 else pltpu.roll(x, by % LANES, 1)


def kernel(
    dims, src_ref, tgt_ref, dual_ref, core_ref, u_out, g_out, core_out,
    srcbuf, tgtall, tgtbuf, dualbuf, corein, lsepair, lsebuf, corepair, corebuf, gbuf, sl, sr, tl, tr, sls, srs, tls, trt, sps, logits, gcol, weighted, ehigh, elow, urow, turned, square,
    send_sem, recv_sem, local_sem,
):
    S, T, rows, cols, fs, ft, feat, ns, nt = dims
    rank = feat + 2
    st = -(-rank // 8) * 8
    jr = cols // LANES
    nr = rows // LANES
    last = 3 + 4 * OUTER
    s, t = lax.axis_index("src"), lax.axis_index("tgt")

    def beside(act):
        for h in range(1, T):
            act(lax.rem(t + h, T))

    def column(act):
        def body(k, unused):
            act(lax.rem(s + k, S))
            return unused

        lax.fori_loop(1, S, body, 0, unroll=S <= 8)

    def remote(phase, src, dst, device):
        return pltpu.make_async_remote_copy(
            src_ref=src, dst_ref=dst, send_sem=send_sem.at[phase], recv_sem=recv_sem.at[phase],
            device_id=device, device_id_type=MESH,
        )

    def bytes_of(phase, slots, count):
        part = slots.at[pl.ds(0, count - 1)]
        return remote(phase, part, part, {"src": lax.rem(s + 1, S)})

    def over_tgt(phase, slots):
        beside(lambda pt: remote(phase, slots.at[t], slots.at[t], {"tgt": pt}).start())

    def over_src(phase, slots):
        column(lambda ps: remote(phase, slots.at[s], slots.at[s], {"src": ps}).start())

    copies = [
        pltpu.make_async_copy(src_ref, srcbuf.at[t, s], local_sem.at[0]),
        pltpu.make_async_copy(tgt_ref, tgtall, local_sem.at[1]),
        pltpu.make_async_copy(dual_ref.at[s], dualbuf, local_sem.at[2]),
        pltpu.make_async_copy(core_ref, corein, local_sem.at[3]),
    ]
    for copy in copies:
        copy.start()
    barrier = pltpu.get_barrier_semaphore()

    def greet(device):
        pl.semaphore_signal(barrier, inc=1, device_id=device, device_id_type=MESH)

    column(lambda ps: greet({"src": ps}))
    beside(lambda pt: greet({"tgt": pt}))
    for copy in copies:
        copy.wait()
    tgtbuf[s] = tgtall[s]
    own_dual = dualbuf[...] * (1.0 / UNIT)
    for r in range(jr):
        gcol[r * LANES : (r + 1) * LANES, :] = jnp.broadcast_to(own_dual[r : r + 1, :], (LANES, LANES)).T
    square[...] = jnp.zeros_like(square)
    square[:rank, :rank] = corein[...]
    turned[...] = square[...].T[:st, :]
    pl.semaphore_wait(barrier, S + T - 2)

    over_src(0, srcbuf.at[t])
    column(lambda ps: remote(1, tgtall.at[ps], tgtbuf.at[s], {"src": ps}).start())
    bytes_of(0, srcbuf.at[t], S).wait_recv()
    over_tgt(2, srcbuf)
    bytes_of(1, tgtbuf, S).wait_recv()

    def lift(ref, values, ahead, scale):
        ref[rank:, :] = jnp.zeros_like(ref[rank:, :])
        squares = jnp.sum(values * values, axis=0, keepdims=True)
        ones = jnp.ones_like(squares)
        ref[0:1, :] = squares if ahead else ones
        ref[1:2, :] = ones if ahead else squares
        ref[2:rank, :] = values if scale is None else scale * values

    def stacked(parts, height):
        width = parts[0].shape[1]
        fill = height - st * len(parts)
        return jnp.concatenate(list(parts) + ([jnp.zeros((fill, width), F32)] if fill else []), axis=0)

    deep = trt.shape[1]
    wide = srs.shape[1]
    for k in range(S):
        for r in range(jr):
            tr[2 + k * ft : 2 + (k + 1) * ft, r * LANES : (r + 1) * LANES] = tgtbuf[k, r * ft : (r + 1) * ft, :]
    lift(tr, tr[2:rank, :], False, None)
    t0, t1, t2 = split3(tr[...])
    trt[...] = stacked((t0, t1, t0, t1, t2, t0), deep).astype(BF16).T

    bytes_of(2, srcbuf, T).wait_recv()
    for k in range(S):
        for h in range(T):
            sr[2 + h * fs : 2 + (h + 1) * fs, k * rows : (k + 1) * rows] = srcbuf[h, k]
    lift(sl, sr[2:rank, :], True, -2.0)
    sls[...] = stacked(split3(sl[...]), wide).astype(BF16)

    per = LANES // st
    block = min(256, ns)
    chunk = min(512, cols)
    def outer(step, unused):
        k0, k1, k2 = split3(turned[...] * (-1.0 / UNIT))
        lhs = stacked(
            (k0 + shifted(k0, st) + shifted(k0, 2 * st), k1 + shifted(k1, st), k2), 3 * st
        ).astype(BF16)
        proj = jnp.dot(lhs, sls[...], preferred_element_type=F32)
        proj = proj[:st] + (proj[st : 2 * st] + proj[2 * st :])
        p0, p1, p2 = split3(proj)
        sps[...] = stacked((p0, p0, p1, p1, p0, p2), deep).astype(BF16)
        sublogs = []
        for b in range(ns // block):
            part = jnp.dot(trt[...], sps[:, b * block : (b + 1) * block], preferred_element_type=F32)
            for h in range(block // LANES):
                at = b * block // LANES + h
                tops = []
                for c in range(cols // chunk):
                    rows_c = slice(c * chunk, (c + 1) * chunk)
                    here = part[rows_c, h * LANES : (h + 1) * LANES] + gcol[rows_c, :]
                    logits[rows_c, at * LANES : (at + 1) * LANES] = here
                    tops.append(jnp.max(here.reshape(chunk // 8, 8, LANES), axis=0))
                top = functools.reduce(jnp.maximum, tops)
                totals = []
                for c in range(cols // chunk):
                    here = logits[c * chunk : (c + 1) * chunk, at * LANES : (at + 1) * LANES]
                    totals.append(jnp.sum(jnp.exp2(here.reshape(chunk // 8, 8, LANES) - top[None]), axis=0))
                sublogs.append(top + jnp.log2(sum(totals)))
        for at in range(ns // LANES):
            top = jnp.max(sublogs[at], axis=0, keepdims=True)
            total = jnp.sum(jnp.exp2(sublogs[at] - top), axis=0, keepdims=True)
            lsepair[step, t, at : at + 1, :] = top + jnp.log2(total)
        phase = 3 + 4 * step
        over_tgt(phase, lsepair.at[step])
        bytes_of(phase, lsepair.at[step], T).wait_recv()
        lsebuf[step, s] = joined(lsepair[step])
        over_src(phase + 1, lsebuf.at[step])

        @pl.when(step == 0)
        def prepare():
            lift(tl, tr[2:rank, :], True, -2.0)
            tls[...] = stacked(split3(tl[...]), wide).astype(BF16)
            lift(sr, sr[2:rank, :], False, None)
            srs[...] = stacked(split3(sr[...]), wide).astype(BF16).T

        bytes_of(phase + 1, lsebuf.at[step], S).wait_recv()
        urow[...] = -math.log2(ns) - joined(lsebuf[step])
        u_all = jnp.concatenate([urow[k : k + 1, :] for k in range(ns // LANES)], axis=1)
        for c in range(cols // chunk):
            sl_c = slice(c * chunk, (c + 1) * chunk)
            starts = range(c * chunk, (c + 1) * chunk, 16)
            tops = [jnp.max(logits[k : k + 16, :] + u_all, axis=1, keepdims=True) for k in starts]
            for k, top in zip(starts, tops):
                e = jnp.exp2((logits[k : k + 16, :] + u_all) - top)
                high = e.astype(BF16)
                ehigh[c, k - c * chunk : k - c * chunk + 16, :] = high
                elow[c, k - c * chunk : k - c * chunk + 16, :] = (e - high.astype(F32)).astype(BF16)
            top = jnp.concatenate(tops, axis=0)
            acc = jnp.dot(ehigh[c], srs[...], preferred_element_type=F32) + jnp.dot(elow[c], srs[...], preferred_element_type=F32)
            total = acc[:, 0:1]
            scaled = acc * (1.0 / total)
            first = scaled.astype(BF16)
            weighted[sl_c, :wide] = first
            weighted[sl_c, wide:] = (scaled - first.astype(F32)).astype(BF16)
            gcol[sl_c, :] = (gcol[sl_c, :] - math.log2(nt)) - (top + jnp.log2(total))
        ext = jnp.dot(tls[...], weighted[...], preferred_element_type=F32)
        ext = ext[:, :wide] + ext[:, wide:]
        kt = ext[:st] + (ext[st : 2 * st] + ext[2 * st : 3 * st])
        kt = kt + (shifted(kt, -st) + shifted(kt, -2 * st))
        kt = lanes_below(kt * (1.0 / nt), st)
        for group in range(corebuf.shape[2] // 8):
            tile = None
            for k in range(per):
                n = group * per + k
                if n * 8 < st:
                    piece = shifted(kt[n * 8 : n * 8 + 8, :], k * st)
                    tile = piece if tile is None else tile + piece
            corepair[step, t, group * 8 : group * 8 + 8, :] = tile
        over_tgt(phase + 2, corepair.at[step])
        bytes_of(phase + 2, corepair.at[step], T).wait_recv()
        corebuf[step, s] = jnp.sum(corepair[step], axis=0)
        over_src(phase + 3, corebuf.at[step])

        @pl.when(step == OUTER - 1)
        def finish_dual():
            for r in range(jr):
                gbuf[s, r : r + 1, :] = gcol[r * LANES : (r + 1) * LANES, :].T[0:1, :] * UNIT
            over_src(last, gbuf)

        bytes_of(phase + 3, corebuf.at[step], S).wait_recv()
        summed = -2.0 * jnp.sum(corebuf[step], axis=0)
        turned[...] = jnp.concatenate(
            [
                lanes_below(shifted(summed[n // per * 8 : n // per * 8 + 8, :], -(n % per) * st), st)
                for n in range(st // 8)
            ],
            axis=0,
        )
        return unused

    lax.fori_loop(0, OUTER, outer, 0)
    u_out[...] = urow[pl.ds(s * nr, nr), :] * UNIT
    square[:st, :] = turned[...]
    core_out[...] = square[...].T[:rank, :rank]

    bytes_of(last, gbuf, S).wait_recv()
    g_out[...] = gbuf[...]
    bytes_of(0, srcbuf.at[t], S).wait_send()
    bytes_of(1, tgtbuf, S).wait_send()
    bytes_of(2, srcbuf, T).wait_send()
    for step in range(OUTER):
        phase = 3 + 4 * step
        bytes_of(phase, lsepair.at[step], T).wait_send()
        bytes_of(phase + 1, lsebuf.at[step], S).wait_send()
        bytes_of(phase + 2, corepair.at[step], T).wait_send()
        bytes_of(phase + 3, corebuf.at[step], S).wait_send()
    bytes_of(last, gbuf, S).wait_send()


def place(*refs):
    count = len(refs) // 2
    for k in range(count):
        refs[count + k][...] = refs[k][...]


def shards(src_feat, tgt_feat, tgt_dual, core_matrix):
    S, T = lax.axis_size("src"), lax.axis_size("tgt")
    rows, fs = src_feat.shape
    held, ft = tgt_feat.shape
    feat = fs * T
    cols = held // S
    ns, nt = rows * S, held * T
    rank = feat + 2
    st = -(-rank // 8) * 8
    jr, nr = cols // LANES, rows // LANES
    per = LANES // st
    groups = -(-(st // 8) // per)
    deep = -(-6 * st // LANES) * LANES
    wide = -(-3 * st // LANES) * LANES
    dims = (S, T, rows, cols, fs, ft, feat, ns, nt)
    chunk = min(512, cols)
    src = src_feat.T
    tgt = tgt_feat.reshape(S * jr, LANES, ft).transpose(0, 2, 1).reshape(S, jr * ft, LANES)
    dual = tgt_dual.reshape(S, jr, LANES)
    phases = 4 + 4 * OUTER
    vmem = pl.BlockSpec(memory_space=pltpu.VMEM)
    u, g, core = pl.pallas_call(
        functools.partial(kernel, dims),
        out_shape=(
            jax.ShapeDtypeStruct((nr, LANES), F32),
            jax.ShapeDtypeStruct((S, jr, LANES), F32),
            jax.ShapeDtypeStruct((rank, rank), F32),
        ),
        in_specs=[pl.BlockSpec(memory_space=pltpu.HBM)] * 4,
        out_specs=(vmem,) * 3,
        scratch_shapes=[
            pltpu.VMEM((T, S, fs, rows), F32),
            pltpu.VMEM((S, jr * ft, LANES), F32),
            pltpu.VMEM((S, jr * ft, LANES), F32),
            pltpu.VMEM((jr, LANES), F32),
            pltpu.VMEM((rank, rank), F32),
            pltpu.VMEM((OUTER, T, ns // LANES, LANES), F32),
            pltpu.VMEM((OUTER, S, ns // LANES, LANES), F32),
            pltpu.VMEM((OUTER, T, groups * 8, LANES), F32),
            pltpu.VMEM((OUTER, S, groups * 8, LANES), F32),
            pltpu.VMEM((S, jr, LANES), F32),
            pltpu.VMEM((st, ns), F32),
            pltpu.VMEM((st, ns), F32),
            pltpu.VMEM((st, cols), F32),
            pltpu.VMEM((st, cols), F32),
            pltpu.VMEM((wide, ns), BF16),
            pltpu.VMEM((ns, wide), BF16),
            pltpu.VMEM((wide, cols), BF16),
            pltpu.VMEM((cols, deep), BF16),
            pltpu.VMEM((deep, ns), BF16),
            pltpu.VMEM((cols, ns), F32),
            pltpu.VMEM((cols, LANES), F32),
            pltpu.VMEM((cols, 2 * wide), BF16),
            pltpu.VMEM((cols // chunk, chunk, ns), BF16),
            pltpu.VMEM((cols // chunk, chunk, ns), BF16),
            pltpu.VMEM((ns // LANES, LANES), F32),
            pltpu.VMEM((st, LANES), F32),
            pltpu.VMEM((LANES, LANES), F32),
            pltpu.SemaphoreType.DMA((phases,)),
            pltpu.SemaphoreType.DMA((phases,)),
            pltpu.SemaphoreType.DMA((4,)),
        ],
        compiler_params=pltpu.CompilerParams(
            collective_id=0, has_side_effects=True, vmem_limit_bytes=64 * 1024 * 1024
        ),
    )(src, tgt, dual, core_matrix)
    placed = [u, g, core]
    u, g, core = pl.pallas_call(
        place,
        out_shape=[jax.ShapeDtypeStruct(x.shape, x.dtype) for x in placed],
        in_specs=[vmem] * 3,
        out_specs=[vmem] * 3,
        compiler_params=pltpu.CompilerParams(vmem_limit_bytes=64 * 1024 * 1024),
    )(*placed)
    return u.reshape(rows), g.reshape(held), core


def solution(mesh):
    placed = (
        P(("pairs", "src"), "tgt"),
        P(("pairs", "tgt"), "src"),
        P(("pairs", "tgt")),
        P("pairs", None),
    )
    return jax.shard_map(
        shards,
        mesh=mesh,
        in_specs=placed,
        out_specs=(P(("pairs", "src")), P(("pairs", "tgt")), P("pairs", None)),
        check_vma=False,
    )
```
